32 devices in a mesh: groups: 2 (over x), rows: 16 (over z, y, core).
Axes of the slice: x: 2, y: 2, z: 4, core: 2. Of those that a mesh axis runs over, the one named last changes fastest.
Arguments:
- context: bfloat16 [256, 256, 256], P(('groups', 'rows')), parts along dimension 0, may hold values from -6 to 6
- conv_weight: bfloat16 [3, 3, 256, 256], replicated, may hold values from -0.125 to 0.125
- conv_bias: float32 [256], replicated, may hold values from -3 to 3
- hr_features: bfloat16 [512, 512, 256], P(('groups', 'rows')), parts along dimension 0, may hold values from -6 to 6
- proj_weight: bfloat16 [512, 256], replicated, may hold values from -0.25 to 0.25
- cot_joined: bfloat16 [512, 512, 256], P(('groups', 'rows')), parts along dimension 0, may hold values from -6 to 6
- cot_context: bfloat16 [256, 256, 256], P(('groups', 'rows')), parts along dimension 0, may hold values from -6 to 6
Outputs:
- joined: bfloat16 [512, 512, 256], P(('groups', 'rows')), parts along dimension 0
- grad_context: float32 [256, 256, 256], P(('groups', 'rows')), parts along dimension 0
- grad_conv_weight: float32 [6, 3, 256, 256], P('groups'), parts along dimension 0
- grad_conv_bias: float32 [512], P('groups'), parts along dimension 0
- grad_proj_weight: float32 [1024, 256], P('groups'), parts along dimension 0
The draws below stay inside these ranges and needn't reach their ends.
There are 2 independent parts, one for each index of `groups`. The reference program is written for one: setup_inputs(seed, part) draws one part's arguments, and reference() takes and returns one part's arrays. A program takes and returns all parts, laid end to end along the dimension named above; an argument that names none is the same for every part. Nothing has to cross between parts.
All inputs are finite; a program needn't handle non-finite values.
Results may differ from the reference program's by a relative error of at most 0.0053.
Values may be sent and summed in bfloat16 or wider, within the bound.
A program may use at most 128 MiB of HBM per device.

```python
import jax
import jax.numpy as jnp
from jax import lax

CHANNELS = 256
CTX_COLS = 256
CTX_ROWS = 128
CROP_ROWS = 32
CROP_COLS = 64
HR_ROWS = 256
HR_COLS = 512


def steps_of(stream_key, shape, split, least, largest):
    gain = 1.0
    for position, parts in split:
        draws = jax.random.uniform(jax.random.fold_in(jax.random.fold_in(stream_key, 6), position), (parts,), jnp.float32, least / len(split), largest / len(split))
        gain = gain * jnp.repeat(jnp.exp(draws), shape[position] // parts).reshape((-1,) + (1,) * (len(shape) - 1 - position))
    return gain


def scatter_about(own_key, dims, width, limit, cuts=(), kind=jnp.bfloat16):
    factor_of = steps_of(own_key, dims, cuts, -0.22, 0.18) if cuts else 1.0
    entries = jax.random.normal(own_key, dims, jnp.float32) * width * factor_of
    return jnp.minimum(jnp.maximum(entries, -limit), limit).astype(kind)


def setup_inputs(seed: int = 0, part: int = 0) -> dict:
    key_list = jax.random.split(jax.random.key(seed), 8)
    part_splits = jax.random.split(jax.random.fold_in(key_list[7], part), 8)
    context = scatter_about(part_splits[0], (CTX_ROWS, CTX_COLS, CHANNELS), 1.0, 6.0, ((0, 16),))
    conv_weight = scatter_about(key_list[1], (3, 3, CHANNELS, CHANNELS), (9 * CHANNELS) ** -0.5, 0.125)
    conv_bias = scatter_about(key_list[2], (CHANNELS,), 0.5, 3.0, (), jnp.float32)
    hr_features = scatter_about(part_splits[3], (HR_ROWS, HR_COLS, CHANNELS), 1.0, 6.0, ((0, 16),))
    proj_weight = scatter_about(key_list[4], (2 * CHANNELS, CHANNELS), (2 * CHANNELS) ** -0.5, 0.25)
    cot_joined = scatter_about(part_splits[5], (HR_ROWS, HR_COLS, CHANNELS), 1.0, 6.0, ((0, 16),))
    cot_context = scatter_about(part_splits[6], (CTX_ROWS, CTX_COLS, CHANNELS), 1.0, 6.0, ((0, 16),))
    return dict(context=context, conv_weight=conv_weight, conv_bias=conv_bias, hr_features=hr_features, proj_weight=proj_weight, cot_joined=cot_joined, cot_context=cot_context)


def silu_grad(values):
    sig = jax.nn.sigmoid(values)
    return sig * (1.0 + values * (1.0 - sig))

def blend_weights(first_row, num_out, anchor, num_in):
    fine_idx = first_row + jnp.arange(num_out, dtype=jnp.int32)
    shifted = 2 * fine_idx - 7
    lower = jnp.floor_divide(shifted, 16)
    frac = (shifted - 16 * lower).astype(jnp.float32) / 16.0
    left_idx = jnp.clip(lower - anchor, 0, num_in - 1)
    right_idx = jnp.clip(lower - anchor + 1, 0, num_in - 1)
    columns = jnp.arange(num_in, dtype=jnp.int32)
    return (1.0 - frac)[:, None] * (columns[None, :] == left_idx[:, None]).astype(jnp.float32) + frac[:, None] * (columns[None, :] == right_idx[:, None]).astype(jnp.float32)

def reference(context, conv_weight, conv_bias, hr_features, proj_weight, cot_joined, cot_context):
    highest = lax.Precision.HIGHEST
    crop_top = 3 * CTX_ROWS // 8
    crop_left = (CTX_COLS - CROP_COLS) // 2
    padded = jnp.pad(context, ((1, 1), (1, 1), (0, 0)))
    preact = jnp.zeros((CTX_ROWS * CTX_COLS, CHANNELS), jnp.float32) + conv_bias
    for row_off in range(3):
        for col_off in range(3):
            window = padded[row_off:row_off + CTX_ROWS, col_off:col_off + CTX_COLS].reshape(-1, CHANNELS)
            preact = preact + jnp.dot(window, conv_weight[row_off, col_off], preferred_element_type=jnp.float32)
    preact = preact.reshape(CTX_ROWS, CTX_COLS, CHANNELS)
    conv_out = (context.astype(jnp.float32) + jax.nn.silu(preact)).astype(jnp.bfloat16)
    crop = conv_out[crop_top:crop_top + CROP_ROWS, crop_left:crop_left + CROP_COLS]
    row_blend = blend_weights(0, HR_ROWS, 0, CROP_ROWS)
    col_blend = blend_weights(0, HR_COLS, 0, CROP_COLS)
    col_mixed = jnp.einsum('xk,jkc->jxc', col_blend, crop.astype(jnp.float32), precision=highest)
    upsampled = jnp.einsum('ij,jxc->ixc', row_blend, col_mixed, precision=highest).astype(jnp.bfloat16)
    combined = jnp.concatenate([hr_features, upsampled], axis=-1).reshape(-1, 2 * CHANNELS)
    projected = jnp.dot(combined, proj_weight, preferred_element_type=jnp.float32)
    joined = jax.nn.silu(projected).astype(jnp.bfloat16).reshape(HR_ROWS, HR_COLS, CHANNELS)
    proj_grad = (cot_joined.reshape(-1, CHANNELS).astype(jnp.float32) * silu_grad(projected)).astype(jnp.bfloat16)
    grad_proj = lax.dot_general(combined, proj_grad, (((0,), (0,)), ((), ())), preferred_element_type=jnp.float32)
    up_grad = lax.dot_general(proj_grad, proj_weight[CHANNELS:], (((1,), (1,)), ((), ())), preferred_element_type=jnp.float32).reshape(HR_ROWS, HR_COLS, CHANNELS)
    row_back = jnp.einsum('ij,ixc->jxc', row_blend, up_grad, precision=highest)
    crop_grad = jnp.einsum('xk,jxc->jkc', col_blend, row_back, precision=highest)
    out_grad = cot_context.astype(jnp.float32) + jnp.pad(crop_grad, ((crop_top, CTX_ROWS - crop_top - CROP_ROWS), (crop_left, CTX_COLS - crop_left - CROP_COLS), (0, 0)))
    pre_grad = (out_grad * silu_grad(preact)).astype(jnp.bfloat16)
    grad_padded = jnp.pad(pre_grad, ((1, 1), (1, 1), (0, 0)))
    pre_flat = pre_grad.reshape(-1, CHANNELS)
    grad_input = out_grad.reshape(-1, CHANNELS)
    kernel_rows = []
    for row_off in range(3):
        kernel_cols = []
        for col_off in range(3):
            window = grad_padded[2 - row_off:2 - row_off + CTX_ROWS, 2 - col_off:2 - col_off + CTX_COLS].reshape(-1, CHANNELS)
            grad_input = grad_input + lax.dot_general(window, conv_weight[row_off, col_off], (((1,), (1,)), ((), ())), preferred_element_type=jnp.float32)
            source = padded[row_off:row_off + CTX_ROWS, col_off:col_off + CTX_COLS].reshape(-1, CHANNELS)
            kernel_cols.append(lax.dot_general(source, pre_flat, (((0,), (0,)), ((), ())), preferred_element_type=jnp.float32))
        kernel_rows.append(jnp.stack(kernel_cols))
    grad_kernel = jnp.stack(kernel_rows)
    grad_bias = lax.optimization_barrier(jnp.sum(pre_grad.astype(jnp.float32), axis=(0, 1)))
    return (joined, grad_input.reshape(CTX_ROWS, CTX_COLS, CHANNELS), grad_kernel, grad_bias, grad_proj)
```

```python
import functools

import jax
import jax.numpy as jnp
from jax import lax
from jax.experimental import pallas as pl
from jax.experimental.pallas import tpu as pltpu
from jax.sharding import PartitionSpec as P

MESH = pl.DeviceIdType.MESH
BF = jnp.bfloat16
F32 = jnp.float32
VMEM_LIMIT = 56 * 1024 * 1024


def dot(lhs, rhs):
    return jnp.dot(lhs, rhs, preferred_element_type=F32)


def dot_t(lhs, rhs):
    return lax.dot_general(lhs, rhs, (((1,), (1,)), ((), ())), preferred_element_type=F32)


def t_dot(lhs, rhs):
    return lax.dot_general(lhs, rhs, (((0,), (0,)), ((), ())), preferred_element_type=F32)


def sigmoid(values):
    return 0.5 * jnp.tanh(0.5 * values) + 0.5


def enter(size):
    group, me = lax.axis_index("groups"), lax.axis_index("rows")
    barrier = pltpu.get_barrier_semaphore()

    def greet(step, carry):
        peer = lax.rem(me + step, size)
        pl.semaphore_signal(barrier, inc=1, device_id=(group, peer), device_id_type=MESH)
        return carry

    lax.fori_loop(1, size, greet, 0)
    pl.semaphore_wait(barrier, size - 1)
    return group, me


def gather_kernel(size, left, width, ctx, cot, c_top, c_bot, g_top, g_bot, crop, send, recv, local):
    group, me = enter(size)
    rows = ctx.shape[0]
    units = rows // 2
    base = 3 * size // 2

    def remote(src, dst, number, slot, peer):
        return pltpu.make_async_remote_copy(
            src_ref=src,
            dst_ref=dst,
            send_sem=send.at[number],
            recv_sem=recv.at[slot],
            device_id=(group, peer),
            device_id_type=MESH,
        )

    def unit(j):
        return ctx.at[pl.ds(2 * j, 2), pl.ds(left, width)]

    def place(k):
        return crop.at[pl.ds(2 * k, 2)]

    sends = []
    for j in range(units):
        index = units * me + j - base
        for k, ok, target in (
            (1, (index >= 0) & (index < size), index),
            (0, index == -1, 0),
            (2, index == size, size - 1),
        ):
            if j != units - 1 and k == 0:
                continue
            if j != 0 and k == 2:
                continue
            copy = remote(unit(j), place(k), len(sends), k, target)
            far = ok & (target != me)
            sends.append((far, copy))
            pl.when(far)(copy.start)
            if k == 1:
                near = pltpu.make_async_copy(unit(j), place(1), local)

                @pl.when(ok & (target == me))
                def _():
                    near.start()
                    near.wait()

    has_up, has_down = me > 0, me < size - 1
    for ok, peer, src, dst, slot in (
        (has_up, me - 1, ctx.at[pl.ds(0, 2)], c_bot, 3),
        (has_down, me + 1, ctx.at[pl.ds(rows - 2, 2)], c_top, 4),
        (has_up, me - 1, cot.at[pl.ds(0, 1)], g_bot, 5),
        (has_down, me + 1, cot.at[pl.ds(rows - 1, 1)], g_top, 6),
    ):
        copy = remote(src, dst, len(sends), slot, peer)
        sends.append((ok, copy))
        pl.when(ok)(copy.start)

    @pl.when(me == 0)
    def _():
        c_top[...] = jnp.zeros_like(c_top)
        g_top[...] = jnp.zeros_like(g_top)

    @pl.when(me == size - 1)
    def _():
        c_bot[...] = jnp.zeros_like(c_bot)
        g_bot[...] = jnp.zeros_like(g_bot)

    mine = (base + me) // units
    take = remote(place(1), place(1), 0, 1, me)
    pl.when(mine != me)(take.wait_recv)
    for ok, peer, k in ((has_up, me - 1, 2), (has_down, me + 1, 0)):
        copy = remote(place(1), place(k), len(sends), k, peer)
        sends.append((ok, copy))
        pl.when(ok)(copy.start)
    for k in (0, 2):
        remote(place(k), place(k), 0, k, me).wait_recv()
    pl.when(has_up)(remote(c_top, c_top, 0, 4, me).wait_recv)
    pl.when(has_up)(remote(g_top, g_top, 0, 6, me).wait_recv)
    pl.when(has_down)(remote(c_bot, c_bot, 0, 3, me).wait_recv)
    pl.when(has_down)(remote(g_bot, g_bot, 0, 5, me).wait_recv)
    for ok, copy in sends:
        pl.when(ok)(copy.wait_send)


def gather(size, context, cot_context, left, width):
    rows, cols, channels = context.shape
    shapes = [(2, cols, channels)] * 2 + [(1, cols, channels)] * 2 + [(6, width, channels)]
    return pl.pallas_call(
        functools.partial(gather_kernel, size, left, width),
        out_shape=[jax.ShapeDtypeStruct(shape, BF) for shape in shapes],
        in_specs=[pl.BlockSpec(memory_space=pl.ANY)] * 2,
        out_specs=[pl.BlockSpec(memory_space=pltpu.VMEM)] * 5,
        scratch_shapes=[
            pltpu.SemaphoreType.DMA((rows // 2 + 8,)),
            pltpu.SemaphoreType.DMA((7,)),
            pltpu.SemaphoreType.DMA,
        ],
        compiler_params=pltpu.CompilerParams(
            collective_id=0, has_side_effects=True, vmem_limit_bytes=VMEM_LIMIT
        ),
    )(context, cot_context)


def fine_kernel(
    size, lead, crop_ctx, conv_w, bias, proj, blend, blend_t, hr, cot,
    joined, wgrad, parts, crop, upper, acc,
):
    step = pl.program_id(0)
    me = lax.axis_index("rows")
    channels = hr.shape[2]
    cols = hr.shape[1]
    narrow, wide = blend.shape[1], crop_ctx.shape[1]
    chunk = 128

    @pl.when(step == 0)
    def _():
        shifted = []
        for b in range(3):
            total = None
            for a in range(3):
                rows = crop_ctx[pl.ds(a, 4)].reshape(4 * wide, channels)
                term = dot(rows, conv_w[a, b])
                total = term if total is None else total + term
            shifted.append(total.reshape(4, wide, channels))
        for row in range(4):
            pre = bias[...] + sum(
                shifted[b][row, lead + b - 1 : lead + b - 1 + narrow] for b in range(3)
            )
            value = crop_ctx[row + 1, lead : lead + narrow].astype(F32) + pre * sigmoid(pre)
            crop[row] = value.astype(BF)

        @pl.when(me == 0)
        def _():
            crop[0] = crop[1]

        @pl.when(me == size - 1)
        def _():
            crop[3] = crop[2]

        for row in range(4):
            coarse = dot(crop[row], proj[pl.ds(channels, channels)]).astype(BF)
            upper[row] = dot(blend[...], coarse)
        acc[...] = jnp.zeros_like(acc)
        wgrad[...] = jnp.zeros_like(wgrad)

    low = (step + 1) // 2
    start = jnp.where(step % 2 == 0, 9, 1)
    weights = [(2 * k + start).astype(F32) * (1.0 / 16.0) for k in range(4)]

    def body(c, carry):
        at = pl.ds(pl.multiple_of(c * chunk, chunk), chunk)
        lo, hi = upper[low, at], upper[low + 1, at]
        x = hr[:, at].reshape(4 * chunk, channels)
        base = dot(x, proj[pl.ds(0, channels)])
        grads = []
        first = second = None
        for k in range(4):
            v = base[k * chunk : (k + 1) * chunk] + (lo + weights[k] * (hi - lo))
            s = sigmoid(v)
            j = v * s
            joined[k, at] = j.astype(BF)
            g = (cot[k, at].astype(F32) * (s + j * (1.0 - s))).astype(BF)
            grads.append(g)
            g = g.astype(F32)
            part = weights[k] * g
            second = part if second is None else second + part
            rest = g - part
            first = rest if first is None else first + rest
        acc[low, at] += first
        acc[low + 1, at] += second
        wgrad[pl.ds(0, channels)] += t_dot(x, jnp.concatenate(grads, axis=0))
        return carry

    lax.fori_loop(0, cols // chunk, body, 0)

    @pl.when(step == pl.num_programs(0) - 1)
    def _():
        back = [dot(blend_t[...], acc[row].astype(BF)) for row in range(4)]
        top = jnp.where(me == 0, 1.0, 0.0)
        bottom = jnp.where(me == size - 1, 1.0, 0.0)
        back[1] = back[1] + top * back[0]
        back[2] = back[2] + bottom * back[3]
        back = [back[0] * (1.0 - top), back[1], back[2], back[3] * (1.0 - bottom)]
        bottom_w = proj[pl.ds(channels, channels)]
        total = None
        for row in range(4):
            low_back = back[row].astype(BF)
            parts[row] = dot_t(low_back, bottom_w)
            term = t_dot(crop[row], low_back)
            total = term if total is None else total + term
        wgrad[pl.ds(channels, channels)] = total


def fine(size, lead, crop_ctx, conv_weight, conv_bias, proj_weight, hr, cot):
    fine_rows, cols, channels = hr.shape
    narrow = cols // 8
    index = 2 * jnp.arange(cols, dtype=jnp.int32) - 7
    lower = jnp.floor_divide(index, 16)
    frac = (index - 16 * lower).astype(F32) / 16.0
    column = jnp.arange(narrow, dtype=jnp.int32)[None, :]
    left = jnp.clip(lower, 0, narrow - 1)[:, None]
    right = jnp.clip(lower + 1, 0, narrow - 1)[:, None]
    blend = (1.0 - frac)[:, None] * (column == left).astype(F32)
    blend = (blend + frac[:, None] * (column == right).astype(F32)).astype(BF)
    whole = lambda shape: pl.BlockSpec(shape, lambda s: (0,) * len(shape))
    tile = pl.BlockSpec((4, cols, channels), lambda s: (s, 0, 0))
    return pl.pallas_call(
        functools.partial(fine_kernel, size, lead),
        grid=(fine_rows // 4,),
        out_shape=[
            jax.ShapeDtypeStruct(hr.shape, BF),
            jax.ShapeDtypeStruct((2 * channels, channels), F32),
            jax.ShapeDtypeStruct((4, narrow, channels), F32),
        ],
        in_specs=[
            whole(crop_ctx.shape),
            whole(conv_weight.shape),
            whole((1, channels)),
            whole(proj_weight.shape),
            whole((cols, narrow)),
            whole((narrow, cols)),
            tile,
            tile,
        ],
        out_specs=[tile, whole((2 * channels, channels)), whole((4, narrow, channels))],
        scratch_shapes=[
            pltpu.VMEM((4, narrow, channels), BF),
            pltpu.VMEM((4, cols, channels), F32),
            pltpu.VMEM((4, cols, channels), F32),
        ],
        compiler_params=pltpu.CompilerParams(vmem_limit_bytes=VMEM_LIMIT),
    )(crop_ctx, conv_weight, conv_bias.reshape(1, -1), proj_weight, blend, blend.T, hr, cot)


def scatter_kernel(size, units, parts, out, up, down, got_up, got_down, mine, send, recv, edge):
    group, me = enter(size)
    base = 3 * size // 2

    def remote(src, dst, s, r, peer):
        return pltpu.make_async_remote_copy(
            src_ref=src,
            dst_ref=dst,
            send_sem=s,
            recv_sem=r,
            device_id=(group, peer),
            device_id_type=MESH,
        )

    has_up, has_down = me > 0, me < size - 1
    up[...] = parts[0].astype(BF)
    down[...] = parts[3].astype(BF)
    to_up = remote(up, got_down, send.at[0], edge.at[0], me - 1)
    to_down = remote(down, got_up, send.at[1], edge.at[1], me + 1)
    pl.when(has_up)(to_up.start)
    pl.when(has_down)(to_down.start)

    @pl.when(me == 0)
    def _():
        got_up[...] = jnp.zeros_like(got_up)

    @pl.when(me == size - 1)
    def _():
        got_down[...] = jnp.zeros_like(got_down)

    for s in range(units + 2):
        index = units * me + s - 1 - base

        @pl.when((index < 0) | (index >= size))
        def _():
            out[s] = jnp.zeros_like(out[s])

    pl.when(has_up)(remote(got_up, got_up, send.at[0], edge.at[1], me).wait_recv)
    pl.when(has_down)(remote(got_down, got_down, send.at[0], edge.at[0], me).wait_recv)
    mine[0] = (parts[1] + got_up[...].astype(F32)).astype(BF)
    mine[1] = (parts[2] + got_down[...].astype(F32)).astype(BF)
    number = base + me
    waits = []
    for s in range(units + 2):
        offset = number + 1 - s
        owner = offset // units
        ok = lax.rem(offset, units) == 0
        copy = remote(mine, out.at[s], send.at[2 + s], recv.at[s], owner)
        far = ok & (owner != me) & (owner >= 0) & (owner < size)
        waits.append((far, copy))
        pl.when(far)(copy.start)

        @pl.when(ok & (owner == me))
        def _():
            out[s] = mine[...]

    for s in range(units + 2):
        index = units * me + s - 1 - base
        here = (index >= 0) & (index < size) & (index != me)
        pl.when(here)(remote(mine, out.at[s], send.at[0], recv.at[s], me).wait_recv)
    for far, copy in waits:
        pl.when(far)(copy.wait_send)
    pl.when(has_up)(to_up.wait_send)
    pl.when(has_down)(to_down.wait_send)


def scatter(size, units, parts):
    _, narrow, channels = parts.shape
    row = (narrow, channels)
    return pl.pallas_call(
        functools.partial(scatter_kernel, size, units),
        out_shape=jax.ShapeDtypeStruct((units + 2, 2) + row, BF),
        in_specs=[pl.BlockSpec(memory_space=pltpu.VMEM)],
        out_specs=pl.BlockSpec(memory_space=pltpu.VMEM),
        scratch_shapes=[pltpu.VMEM(row, BF)] * 4
        + [
            pltpu.VMEM((2,) + row, BF),
            pltpu.SemaphoreType.DMA((units + 4,)),
            pltpu.SemaphoreType.DMA((units + 2,)),
            pltpu.SemaphoreType.DMA((2,)),
        ],
        compiler_params=pltpu.CompilerParams(
            collective_id=1, has_side_effects=True, vmem_limit_bytes=VMEM_LIMIT
        ),
    )(parts)


def coarse_kernel(
    left, ctx, c_top, c_bot, cot, g_top, g_bot, crop_grad, conv_w, bias,
    grad, wgrad, bgrad, ext, ext_t, outg, pre_g,
):
    rows, cols, channels = ctx.shape
    narrow = crop_grad.shape[1]
    ext[pl.ds(0, 2)] = c_top[...]
    ext[pl.ds(2, rows)] = ctx[...]
    ext[pl.ds(rows + 2, 2)] = c_bot[...]
    outg[pl.ds(0, 1)] = g_top[...].astype(F32)
    outg[pl.ds(1, rows)] = cot[...].astype(F32)
    outg[pl.ds(rows + 1, 1)] = g_bot[...].astype(F32)
    for r in range(rows + 2):
        outg[r, pl.ds(left, narrow)] += crop_grad[r + 1].astype(F32)
    column = lax.broadcasted_iota(jnp.int32, (cols, channels), 0)

    def later(v):
        return jnp.where(column == 0, 0.0, pltpu.roll(v, 1, 0))

    def sooner(v):
        return jnp.where(column == cols - 1, 0.0, pltpu.roll(v, cols - 1, 0))

    def turn(r, carry):
        ext_t[r] = jnp.transpose(ext[r + 1])
        return carry

    lax.fori_loop(0, rows + 2, turn, 0)
    bgrad[...] = jnp.zeros_like(bgrad)

    def forward(p, carry):
        sums = []
        for b in range(3):
            total = None
            for a in range(3):
                term = dot(ext[pl.ds(2 * p + a, 2)].reshape(2 * cols, channels), conv_w[a, b])
                total = term if total is None else total + term
            sums.append(total)
        for k in range(2):
            cut = slice(k * cols, (k + 1) * cols)
            r = 2 * p + k
            v = bias[...] + later(sums[0][cut]) + sums[1][cut] + sooner(sums[2][cut])
            s = sigmoid(v)
            g = (outg[r] * (s * (1.0 + v * (1.0 - s)))).astype(BF)
            pre_g[1, r] = g
            g = g.astype(F32)
            pre_g[0, r] = sooner(g).astype(BF)
            pre_g[2, r] = later(g).astype(BF)
            own = ((r >= 1) & (r <= rows)).astype(F32)
            bgrad[...] += own * jnp.sum(g, axis=0, keepdims=True)
        return carry

    lax.fori_loop(0, (rows + 2) // 2, forward, 0)

    def backward(p, carry):
        sums = []
        for b in range(3):
            total = None
            for a in range(3):
                term = dot_t(
                    pre_g[1, pl.ds(2 * p + 2 - a, 2)].reshape(2 * cols, channels), conv_w[a, b]
                )
                total = term if total is None else total + term
            sums.append(total)
        for k in range(2):
            cut = slice(k * cols, (k + 1) * cols)
            r = 2 * p + k
            grad[r] = outg[r + 1] + (sooner(sums[0][cut]) + sums[1][cut] + later(sums[2][cut]))
        return carry

    lax.fori_loop(0, rows // 2, backward, 0)

    def weights(n, carry):
        a, b = n // 3, n % 3
        total = None
        for i in range(rows):
            term = dot(ext_t[i + a], pre_g[b, i + 1])
            total = term if total is None else total + term
        wgrad[n] = total
        return carry

    lax.fori_loop(0, 9, weights, 0)


def coarse(left, context, halos, cot_context, crop_grad, conv_weight, conv_bias):
    rows, cols, channels = context.shape
    c_top, c_bot, g_top, g_bot = halos
    return pl.pallas_call(
        functools.partial(coarse_kernel, left),
        out_shape=[
            jax.ShapeDtypeStruct((rows, cols, channels), F32),
            jax.ShapeDtypeStruct((9, channels, channels), F32),
            jax.ShapeDtypeStruct((1, channels), F32),
        ],
        in_specs=[pl.BlockSpec(memory_space=pltpu.VMEM)] * 9,
        out_specs=[pl.BlockSpec(memory_space=pltpu.VMEM)] * 3,
        scratch_shapes=[
            pltpu.VMEM((rows + 4, cols, channels), BF),
            pltpu.VMEM((rows + 2, channels, cols), BF),
            pltpu.VMEM((rows + 2, cols, channels), F32),
            pltpu.VMEM((3, rows + 2, cols, channels), BF),
        ],
        compiler_params=pltpu.CompilerParams(vmem_limit_bytes=VMEM_LIMIT),
    )(context, c_top, c_bot, cot_context, g_top, g_bot, crop_grad, conv_weight,
      conv_bias.reshape(1, -1))


def per_device(size, context, conv_weight, conv_bias, hr_features, proj_weight, cot_joined,
               cot_context):
    rows, cols, channels = context.shape
    narrow = hr_features.shape[1] // 8
    left = (cols - narrow) // 2
    lead = 16
    *halos, crop_ctx = gather(size, context, cot_context, left - lead, narrow + 2 * lead)
    joined, proj_grad, parts = fine(
        size, lead, crop_ctx, conv_weight, conv_bias, proj_weight, hr_features, cot_joined
    )
    crop_grad = scatter(size, rows // 2, parts).reshape(-1, narrow, channels)
    grad, conv_grad, bias_grad = coarse(
        left, context, halos, cot_context, crop_grad, conv_weight, conv_bias
    )
    conv_grad, bias_grad, proj_grad = lax.psum((conv_grad, bias_grad, proj_grad), "rows")
    return (
        joined,
        grad,
        conv_grad.reshape(3, 3, channels, channels),
        bias_grad.reshape(-1),
        proj_grad,
    )


def solution(mesh):
    tile = P(("groups", "rows"), None, None)
    return jax.shard_map(
        functools.partial(per_device, mesh.shape["rows"]),
        mesh=mesh,
        in_specs=(tile, P(), P(), tile, P(), tile, tile),
        out_specs=(tile, tile, P("groups", None, None, None), P("groups"), P("groups", None)),
        check_vma=False,
    )
```

```python
import functools

import jax
import jax.numpy as jnp
from jax import lax
from jax.experimental import pallas as pl
from jax.experimental.pallas import tpu as pltpu
from jax.sharding import PartitionSpec as P

MESH = pl.DeviceIdType.MESH
BF = jnp.bfloat16
F32 = jnp.float32
VMEM_LIMIT = 56 * 1024 * 1024


def dot(lhs, rhs):
    return jnp.dot(lhs, rhs, preferred_element_type=F32)


def dot_t(lhs, rhs):
    return lax.dot_general(lhs, rhs, (((1,), (1,)), ((), ())), preferred_element_type=F32)


def t_dot(lhs, rhs):
    return lax.dot_general(lhs, rhs, (((0,), (0,)), ((), ())), preferred_element_type=F32)


def sigmoid(values):
    return 0.5 * jnp.tanh(0.5 * values) + 0.5


def enter(size):
    group, me = lax.axis_index("groups"), lax.axis_index("rows")
    barrier = pltpu.get_barrier_semaphore()

    def greet(step, carry):
        peer = lax.rem(me + step, size)
        pl.semaphore_signal(barrier, inc=1, device_id=(group, peer), device_id_type=MESH)
        return carry

    lax.fori_loop(1, size, greet, 0)
    pl.semaphore_wait(barrier, size - 1)
    return group, me


def gather_kernel(size, left, width, ctx, cot, c_top, c_bot, g_top, g_bot, crop, send, recv, local):
    group, me = enter(size)
    rows = ctx.shape[0]
    units = rows // 2
    base = 3 * size // 2

    def remote(src, dst, number, slot, peer):
        return pltpu.make_async_remote_copy(
            src_ref=src,
            dst_ref=dst,
            send_sem=send.at[number],
            recv_sem=recv.at[slot],
            device_id=(group, peer),
            device_id_type=MESH,
        )

    def unit(j):
        return ctx.at[pl.ds(2 * j, 2), pl.ds(left, width)]

    def place(k):
        return crop.at[pl.ds(2 * k, 2)]

    sends = []
    for j in range(units):
        index = units * me + j - base
        for k, ok, target in (
            (1, (index >= 0) & (index < size), index),
            (0, index == -1, 0),
            (2, index == size, size - 1),
        ):
            if j != units - 1 and k == 0:
                continue
            if j != 0 and k == 2:
                continue
            copy = remote(unit(j), place(k), len(sends), k, target)
            far = ok & (target != me)
            sends.append((far, copy))
            pl.when(far)(copy.start)
            if k == 1:
                near = pltpu.make_async_copy(unit(j), place(1), local)

                @pl.when(ok & (target == me))
                def _():
                    near.start()
                    near.wait()

    has_up, has_down = me > 0, me < size - 1
    for ok, peer, src, dst, slot in (
        (has_up, me - 1, ctx.at[pl.ds(0, 2)], c_bot, 3),
        (has_down, me + 1, ctx.at[pl.ds(rows - 2, 2)], c_top, 4),
        (has_up, me - 1, cot.at[pl.ds(0, 1)], g_bot, 5),
        (has_down, me + 1, cot.at[pl.ds(rows - 1, 1)], g_top, 6),
    ):
        copy = remote(src, dst, len(sends), slot, peer)
        sends.append((ok, copy))
        pl.when(ok)(copy.start)

    @pl.when(me == 0)
    def _():
        c_top[...] = jnp.zeros_like(c_top)
        g_top[...] = jnp.zeros_like(g_top)

    @pl.when(me == size - 1)
    def _():
        c_bot[...] = jnp.zeros_like(c_bot)
        g_bot[...] = jnp.zeros_like(g_bot)

    mine = (base + me) // units
    take = remote(place(1), place(1), 0, 1, me)
    pl.when(mine != me)(take.wait_recv)
    for ok, peer, k in ((has_up, me - 1, 2), (has_down, me + 1, 0)):
        copy = remote(place(1), place(k), len(sends), k, peer)
        sends.append((ok, copy))
        pl.when(ok)(copy.start)
    for k in (0, 2):
        remote(place(k), place(k), 0, k, me).wait_recv()
    pl.when(has_up)(remote(c_top, c_top, 0, 4, me).wait_recv)
    pl.when(has_up)(remote(g_top, g_top, 0, 6, me).wait_recv)
    pl.when(has_down)(remote(c_bot, c_bot, 0, 3, me).wait_recv)
    pl.when(has_down)(remote(g_bot, g_bot, 0, 5, me).wait_recv)
    for ok, copy in sends:
        pl.when(ok)(copy.wait_send)


def gather(size, context, cot_context, left, width):
    rows, cols, channels = context.shape
    shapes = [(2, cols, channels)] * 2 + [(1, cols, channels)] * 2 + [(6, width, channels)]
    return pl.pallas_call(
        functools.partial(gather_kernel, size, left, width),
        out_shape=[jax.ShapeDtypeStruct(shape, BF) for shape in shapes],
        in_specs=[pl.BlockSpec(memory_space=pl.ANY)] * 2,
        out_specs=[pl.BlockSpec(memory_space=pltpu.VMEM)] * 5,
        scratch_shapes=[
            pltpu.SemaphoreType.DMA((rows // 2 + 8,)),
            pltpu.SemaphoreType.DMA((7,)),
            pltpu.SemaphoreType.DMA,
        ],
        compiler_params=pltpu.CompilerParams(
            collective_id=0, has_side_effects=True, vmem_limit_bytes=VMEM_LIMIT
        ),
    )(context, cot_context)


def fine_kernel(
    size, lead, crop_ctx, conv_w, bias, proj, blend, blend_t, hr, cot,
    joined, wgrad, parts, crop, upper, acc,
):
    step = pl.program_id(0)
    me = lax.axis_index("rows")
    channels = hr.shape[2]
    cols = hr.shape[1]
    narrow, wide = blend.shape[1], crop_ctx.shape[1]
    chunk = 128

    @pl.when(step == 0)
    def _():
        shifted = []
        for b in range(3):
            total = None
            for a in range(3):
                rows = crop_ctx[pl.ds(a, 4)].reshape(4 * wide, channels)
                term = dot(rows, conv_w[a, b])
                total = term if total is None else total + term
            shifted.append(total.reshape(4, wide, channels))
        for row in range(4):
            pre = bias[...] + sum(
                shifted[b][row, lead + b - 1 : lead + b - 1 + narrow] for b in range(3)
            )
            value = crop_ctx[row + 1, lead : lead + narrow].astype(F32) + pre * sigmoid(pre)
            crop[row] = value.astype(BF)

        @pl.when(me == 0)
        def _():
            crop[0] = crop[1]

        @pl.when(me == size - 1)
        def _():
            crop[3] = crop[2]

        for row in range(4):
            coarse = dot(crop[row], proj[pl.ds(channels, channels)]).astype(BF)
            upper[row] = dot(blend[...], coarse)
        acc[...] = jnp.zeros_like(acc)
        wgrad[...] = jnp.zeros_like(wgrad)

    low = (step + 1) // 2
    start = jnp.where(step % 2 == 0, 9, 1)
    weights = [(2 * k + start).astype(F32) * (1.0 / 16.0) for k in range(4)]

    def body(c, carry):
        at = pl.ds(pl.multiple_of(c * chunk, chunk), chunk)
        lo, hi = upper[low, at], upper[low + 1, at]
        x = hr[:, at].reshape(4 * chunk, channels)
        base = dot(x, proj[pl.ds(0, channels)])
        grads = []
        first = second = None
        for k in range(4):
            v = base[k * chunk : (k + 1) * chunk] + (lo + weights[k] * (hi - lo))
            s = sigmoid(v)
            j = v * s
            joined[k, at] = j.astype(BF)
            g = (cot[k, at].astype(F32) * (s + j * (1.0 - s))).astype(BF)
            grads.append(g)
            g = g.astype(F32)
            part = weights[k] * g
            second = part if second is None else second + part
            rest = g - part
            first = rest if first is None else first + rest
        acc[low, at] += first
        acc[low + 1, at] += second
        wgrad[pl.ds(0, channels)] += t_dot(x, jnp.concatenate(grads, axis=0))
        return carry

    lax.fori_loop(0, cols // chunk, body, 0)

    @pl.when(step == pl.num_programs(0) - 1)
    def _():
        back = [dot(blend_t[...], acc[row].astype(BF)) for row in range(4)]
        top = jnp.where(me == 0, 1.0, 0.0)
        bottom = jnp.where(me == size - 1, 1.0, 0.0)
        back[1] = back[1] + top * back[0]
        back[2] = back[2] + bottom * back[3]
        back = [back[0] * (1.0 - top), back[1], back[2], back[3] * (1.0 - bottom)]
        bottom_w = proj[pl.ds(channels, channels)]
        total = None
        for row in range(4):
            low_back = back[row].astype(BF)
            parts[row] = dot_t(low_back, bottom_w)
            term = t_dot(crop[row], low_back)
            total = term if total is None else total + term
        wgrad[pl.ds(channels, channels)] = total


def fine(size, lead, crop_ctx, conv_weight, conv_bias, proj_weight, hr, cot):
    fine_rows, cols, channels = hr.shape
    narrow = cols // 8
    index = 2 * jnp.arange(cols, dtype=jnp.int32) - 7
    lower = jnp.floor_divide(index, 16)
    frac = (index - 16 * lower).astype(F32) / 16.0
    column = jnp.arange(narrow, dtype=jnp.int32)[None, :]
    left = jnp.clip(lower, 0, narrow - 1)[:, None]
    right = jnp.clip(lower + 1, 0, narrow - 1)[:, None]
    blend = (1.0 - frac)[:, None] * (column == left).astype(F32)
    blend = (blend + frac[:, None] * (column == right).astype(F32)).astype(BF)
    whole = lambda shape: pl.BlockSpec(shape, lambda s: (0,) * len(shape))
    tile = pl.BlockSpec((4, cols, channels), lambda s: (s, 0, 0))
    return pl.pallas_call(
        functools.partial(fine_kernel, size, lead),
        grid=(fine_rows // 4,),
        out_shape=[
            jax.ShapeDtypeStruct(hr.shape, BF),
            jax.ShapeDtypeStruct((2 * channels, channels), F32),
            jax.ShapeDtypeStruct((4, narrow, channels), F32),
        ],
        in_specs=[
            whole(crop_ctx.shape),
            whole(conv_weight.shape),
            whole((1, channels)),
            whole(proj_weight.shape),
            whole((cols, narrow)),
            whole((narrow, cols)),
            tile,
            tile,
        ],
        out_specs=[tile, whole((2 * channels, channels)), whole((4, narrow, channels))],
        scratch_shapes=[
            pltpu.VMEM((4, narrow, channels), BF),
            pltpu.VMEM((4, cols, channels), F32),
            pltpu.VMEM((4, cols, channels), F32),
        ],
        compiler_params=pltpu.CompilerParams(vmem_limit_bytes=VMEM_LIMIT),
    )(crop_ctx, conv_weight, conv_bias.reshape(1, -1), proj_weight, blend, blend.T, hr, cot)


def scatter_kernel(size, units, parts, out, up, down, got_up, got_down, mine, send, recv, edge):
    group, me = enter(size)
    base = 3 * size // 2

    def remote(src, dst, s, r, peer):
        return pltpu.make_async_remote_copy(
            src_ref=src,
            dst_ref=dst,
            send_sem=s,
            recv_sem=r,
            device_id=(group, peer),
            device_id_type=MESH,
        )

    has_up, has_down = me > 0, me < size - 1
    up[...] = parts[0].astype(BF)
    down[...] = parts[3].astype(BF)
    to_up = remote(up, got_down, send.at[0], edge.at[0], me - 1)
    to_down = remote(down, got_up, send.at[1], edge.at[1], me + 1)
    pl.when(has_up)(to_up.start)
    pl.when(has_down)(to_down.start)

    @pl.when(me == 0)
    def _():
        got_up[...] = jnp.zeros_like(got_up)

    @pl.when(me == size - 1)
    def _():
        got_down[...] = jnp.zeros_like(got_down)

    for s in range(units + 2):
        index = units * me + s - 1 - base

        @pl.when((index < 0) | (index >= size))
        def _():
            out[s] = jnp.zeros_like(out[s])

    pl.when(has_up)(remote(got_up, got_up, send.at[0], edge.at[1], me).wait_recv)
    pl.when(has_down)(remote(got_down, got_down, send.at[0], edge.at[0], me).wait_recv)
    mine[0] = (parts[1] + got_up[...].astype(F32)).astype(BF)
    mine[1] = (parts[2] + got_down[...].astype(F32)).astype(BF)
    number = base + me
    waits = []
    for s in range(units + 2):
        offset = number + 1 - s
        owner = offset // units
        ok = lax.rem(offset, units) == 0
        copy = remote(mine, out.at[s], send.at[2 + s], recv.at[s], owner)
        far = ok & (owner != me) & (owner >= 0) & (owner < size)
        waits.append((far, copy))
        pl.when(far)(copy.start)

        @pl.when(ok & (owner == me))
        def _():
            out[s] = mine[...]

    for s in range(units + 2):
        index = units * me + s - 1 - base
        here = (index >= 0) & (index < size) & (index != me)
        pl.when(here)(remote(mine, out.at[s], send.at[0], recv.at[s], me).wait_recv)
    for far, copy in waits:
        pl.when(far)(copy.wait_send)
    pl.when(has_up)(to_up.wait_send)
    pl.when(has_down)(to_down.wait_send)


def scatter(size, units, parts):
    _, narrow, channels = parts.shape
    row = (narrow, channels)
    return pl.pallas_call(
        functools.partial(scatter_kernel, size, units),
        out_shape=jax.ShapeDtypeStruct((units + 2, 2) + row, BF),
        in_specs=[pl.BlockSpec(memory_space=pltpu.VMEM)],
        out_specs=pl.BlockSpec(memory_space=pltpu.VMEM),
        scratch_shapes=[pltpu.VMEM(row, BF)] * 4
        + [
            pltpu.VMEM((2,) + row, BF),
            pltpu.SemaphoreType.DMA((units + 4,)),
            pltpu.SemaphoreType.DMA((units + 2,)),
            pltpu.SemaphoreType.DMA((2,)),
        ],
        compiler_params=pltpu.CompilerParams(
            collective_id=1, has_side_effects=True, vmem_limit_bytes=VMEM_LIMIT
        ),
    )(parts)


def coarse_kernel(
    left, ctx, c_top, c_bot, cot, g_top, g_bot, crop_grad, conv_w, bias,
    grad, wgrad, bgrad, ext, ext_t, outg, pre_g,
):
    rows, cols, channels = ctx.shape
    narrow = crop_grad.shape[1]
    ext[pl.ds(0, 2)] = c_top[...]
    ext[pl.ds(2, rows)] = ctx[...]
    ext[pl.ds(rows + 2, 2)] = c_bot[...]
    outg[pl.ds(0, 1)] = g_top[...].astype(F32)
    outg[pl.ds(1, rows)] = cot[...].astype(F32)
    outg[pl.ds(rows + 1, 1)] = g_bot[...].astype(F32)
    for r in range(rows + 2):
        outg[r, pl.ds(left, narrow)] += crop_grad[r + 1].astype(F32)
    column = lax.broadcasted_iota(jnp.int32, (cols, channels), 0)

    def later(v):
        return jnp.where(column == 0, 0.0, pltpu.roll(v, 1, 0))

    def sooner(v):
        return jnp.where(column == cols - 1, 0.0, pltpu.roll(v, cols - 1, 0))

    def turn(r, carry):
        ext_t[r] = jnp.transpose(ext[r + 1])
        return carry

    lax.fori_loop(0, rows + 2, turn, 0)
    bgrad[...] = jnp.zeros_like(bgrad)

    def forward(p, carry):
        sums = []
        for b in range(3):
            total = None
            for a in range(3):
                term = dot(ext[pl.ds(2 * p + a, 2)].reshape(2 * cols, channels), conv_w[a, b])
                total = term if total is None else total + term
            sums.append(total)
        for k in range(2):
            cut = slice(k * cols, (k + 1) * cols)
            r = 2 * p + k
            v = bias[...] + later(sums[0][cut]) + sums[1][cut] + sooner(sums[2][cut])
            s = sigmoid(v)
            g = (outg[r] * (s * (1.0 + v * (1.0 - s)))).astype(BF)
            pre_g[1, r] = g
            g = g.astype(F32)
            pre_g[0, r] = sooner(g).astype(BF)
            pre_g[2, r] = later(g).astype(BF)
            own = ((r >= 1) & (r <= rows)).astype(F32)
            bgrad[pl.ds(0, 1)] += own * jnp.sum(g, axis=0, keepdims=True)
        return carry

    lax.fori_loop(0, (rows + 2) // 2, forward, 0)

    def backward(p, carry):
        sums = []
        for b in range(3):
            total = None
            for a in range(3):
                term = dot_t(
                    pre_g[1, pl.ds(2 * p + 2 - a, 2)].reshape(2 * cols, channels), conv_w[a, b]
                )
                total = term if total is None else total + term
            sums.append(total)
        for k in range(2):
            cut = slice(k * cols, (k + 1) * cols)
            r = 2 * p + k
            grad[r] = outg[r + 1] + (sooner(sums[0][cut]) + sums[1][cut] + later(sums[2][cut]))
        return carry

    lax.fori_loop(0, rows // 2, backward, 0)

    def weights(n, carry):
        a, b = n // 3, n % 3
        total = None
        for i in range(rows):
            term = dot(ext_t[i + a], pre_g[b, i + 1])
            total = term if total is None else total + term
        wgrad[n] = total
        return carry

    lax.fori_loop(0, 9, weights, 0)


def coarse(left, context, halos, cot_context, crop_grad, conv_weight, conv_bias):
    rows, cols, channels = context.shape
    c_top, c_bot, g_top, g_bot = halos
    return pl.pallas_call(
        functools.partial(coarse_kernel, left),
        out_shape=[
            jax.ShapeDtypeStruct((rows, cols, channels), F32),
            jax.ShapeDtypeStruct((9, channels, channels), F32),
            jax.ShapeDtypeStruct((8, channels), F32),
        ],
        in_specs=[pl.BlockSpec(memory_space=pltpu.VMEM)] * 9,
        out_specs=[pl.BlockSpec(memory_space=pltpu.VMEM)] * 3,
        scratch_shapes=[
            pltpu.VMEM((rows + 4, cols, channels), BF),
            pltpu.VMEM((rows + 2, channels, cols), BF),
            pltpu.VMEM((rows + 2, cols, channels), F32),
            pltpu.VMEM((3, rows + 2, cols, channels), BF),
        ],
        compiler_params=pltpu.CompilerParams(vmem_limit_bytes=VMEM_LIMIT),
    )(context, c_top, c_bot, cot_context, g_top, g_bot, crop_grad, conv_weight,
      conv_bias.reshape(1, -1))


def reduce_kernel(size, conv, proj, bias, out, acc, outgoing, incoming, send, recv, back, load):
    group, me = lax.axis_index("groups"), lax.axis_index("rows")
    total_rows, channels = acc.shape
    half = channels // 2
    bits = [2**k for k in range(size.bit_length() - 1)]
    orders = (bits, bits[:1] + bits[2:] + bits[1:2])
    steps = len(bits)
    n_conv, n_proj, n_bias = conv.shape[0], proj.shape[0], bias.shape[0]
    loads = [
        pltpu.make_async_copy(conv, acc.at[pl.ds(0, n_conv)], load.at[0]),
        pltpu.make_async_copy(proj, acc.at[pl.ds(n_conv, n_proj)], load.at[1]),
        pltpu.make_async_copy(bias, acc.at[pl.ds(n_conv + n_proj, n_bias)], load.at[2]),
    ]
    for copy in loads:
        copy.start()
    used = n_conv + n_proj + n_bias
    acc[pl.ds(used, total_rows - used)] = jnp.zeros((total_rows - used, channels), F32)

    def side(bit):
        return lax.rem(me // bit, 2)

    def partner(bit):
        return me + bit * (1 - 2 * side(bit))

    barrier = pltpu.get_barrier_semaphore()
    for bit in bits:
        pl.semaphore_signal(barrier, inc=1, device_id=(group, partner(bit)), device_id_type=MESH)
    pl.semaphore_wait(barrier, steps)
    for copy in loads:
        copy.wait()

    def remote(src, dst, s, r, bit):
        return pltpu.make_async_remote_copy(
            src_ref=src,
            dst_ref=dst,
            send_sem=s,
            recv_sem=r,
            device_id=(group, partner(bit)),
            device_id_type=MESH,
        )

    def rows_at(start, count):
        return pl.ds(pl.multiple_of(start, 16), count)

    low = [0, 0]
    kept = [[], []]
    copies = []
    pending = [None, None]
    for step in range(steps + 1):
        for h in range(2):
            lanes = pl.ds(h * half, half)
            if step > 0:
                count = total_rows >> step
                pending[h].wait_recv()
                got = incoming[pl.ds(total_rows - 2 * count, count), lanes]
                acc[rows_at(low[h], count), lanes] += got.astype(F32)
            if step < steps:
                bit = orders[h][step]
                count = total_rows >> (step + 1)
                mine = low[h] + side(bit) * count
                other = low[h] + (1 - side(bit)) * count
                there = rows_at(other, count)
                outgoing[there, lanes] = acc[there, lanes].astype(BF)
                copy = remote(
                    outgoing.at[there, lanes],
                    incoming.at[pl.ds(total_rows - 2 * count, count), lanes],
                    send.at[h, step],
                    recv.at[h, step],
                    bit,
                )
                copy.start()
                copies.append(copy)
                pending[h] = copy
                low[h] = mine
                kept[h].append(mine)
            else:
                here = rows_at(low[h], total_rows >> steps)
                out[here, lanes] = acc[here, lanes].astype(BF)
                bit = orders[h][steps - 1]
                copy = remote(
                    out.at[here, lanes],
                    out.at[here, lanes],
                    send.at[h, steps],
                    back.at[h, steps - 1],
                    bit,
                )
                copy.start()
                copies.append(copy)
                pending[h] = copy
    for step in reversed(range(steps)):
        for h in range(2):
            lanes = pl.ds(h * half, half)
            pending[h].wait_recv()
            if step > 0:
                here = rows_at(kept[h][step - 1], total_rows >> step)
                copy = remote(
                    out.at[here, lanes],
                    out.at[here, lanes],
                    send.at[h, 2 * steps - step],
                    back.at[h, step - 1],
                    orders[h][step - 1],
                )
                copy.start()
                copies.append(copy)
                pending[h] = copy
    for copy in copies:
        copy.wait_send()


def reduce_sums(size, conv, proj, bias):
    channels = conv.shape[1]
    rows = conv.shape[0] + proj.shape[0] + bias.shape[0]
    rows = -(-rows // (16 * size)) * 16 * size
    steps = size.bit_length() - 1
    return pl.pallas_call(
        functools.partial(reduce_kernel, size),
        out_shape=jax.ShapeDtypeStruct((rows, channels), BF),
        in_specs=[pl.BlockSpec(memory_space=pl.ANY)] * 3,
        out_specs=pl.BlockSpec(memory_space=pltpu.VMEM),
        scratch_shapes=[
            pltpu.VMEM((rows, channels), F32),
            pltpu.VMEM((rows, channels), BF),
            pltpu.VMEM((rows, channels), BF),
            pltpu.SemaphoreType.DMA((2, 2 * steps)),
            pltpu.SemaphoreType.DMA((2, steps)),
            pltpu.SemaphoreType.DMA((2, steps)),
            pltpu.SemaphoreType.DMA((3,)),
        ],
        compiler_params=pltpu.CompilerParams(
            collective_id=2, has_side_effects=True, vmem_limit_bytes=VMEM_LIMIT
        ),
    )(conv, proj, bias)


def per_device(size, context, conv_weight, conv_bias, hr_features, proj_weight, cot_joined,
               cot_context):
    rows, cols, channels = context.shape
    narrow = hr_features.shape[1] // 8
    left = (cols - narrow) // 2
    lead = 16
    *halos, crop_ctx = gather(size, context, cot_context, left - lead, narrow + 2 * lead)
    joined, proj_grad, parts = fine(
        size, lead, crop_ctx, conv_weight, conv_bias, proj_weight, hr_features, cot_joined
    )
    crop_grad = scatter(size, rows // 2, parts).reshape(-1, narrow, channels)
    grad, conv_grad, bias_grad = coarse(
        left, context, halos, cot_context, crop_grad, conv_weight, conv_bias
    )
    sums = reduce_sums(size, conv_grad.reshape(-1, channels), proj_grad, bias_grad).astype(F32)
    first, second = 9 * channels, 11 * channels
    return (
        joined,
        grad,
        sums[:first].reshape(3, 3, channels, channels),
        sums[second],
        sums[first:second],
    )


def solution(mesh):
    tile = P(("groups", "rows"), None, None)
    return jax.shard_map(
        functools.partial(per_device, mesh.shape["rows"]),
        mesh=mesh,
        in_specs=(tile, P(), P(), tile, P(), tile, tile),
        out_specs=(tile, tile, P("groups", None, None, None), P("groups"), P("groups", None)),
        check_vma=False,
    )
```

```python
import functools

import jax
import jax.numpy as jnp
import numpy as np
from jax import lax
from jax.experimental import pallas as pl
from jax.experimental.pallas import tpu as pltpu
from jax.sharding import PartitionSpec as P

MESH = pl.DeviceIdType.MESH
BF = jnp.bfloat16
F32 = jnp.float32
VMEM_LIMIT = 56 * 1024 * 1024


def dot(lhs, rhs):
    return jnp.dot(lhs, rhs, preferred_element_type=F32)


def dot_t(lhs, rhs):
    return lax.dot_general(lhs, rhs, (((1,), (1,)), ((), ())), preferred_element_type=F32)


def t_dot(lhs, rhs):
    return lax.dot_general(lhs, rhs, (((0,), (0,)), ((), ())), preferred_element_type=F32)


def sigmoid(values):
    return 0.5 * jnp.tanh(0.5 * values) + 0.5


def enter(size):
    group, me = lax.axis_index("groups"), lax.axis_index("rows")
    barrier = pltpu.get_barrier_semaphore()

    def greet(step, carry):
        peer = lax.rem(me + step, size)
        pl.semaphore_signal(barrier, inc=1, device_id=(group, peer), device_id_type=MESH)
        return carry

    lax.fori_loop(1, size, greet, 0)
    pl.semaphore_wait(barrier, size - 1)
    return group, me


def gather_kernel(size, left, width, ctx, cot, c_top, c_bot, g_top, g_bot, crop, send, recv, local):
    group, me = enter(size)
    rows = ctx.shape[0]
    units = rows // 2
    base = 3 * size // 2

    def remote(src, dst, number, slot, peer):
        return pltpu.make_async_remote_copy(
            src_ref=src,
            dst_ref=dst,
            send_sem=send.at[number],
            recv_sem=recv.at[slot],
            device_id=(group, peer),
            device_id_type=MESH,
        )

    def unit(j):
        return ctx.at[pl.ds(2 * j, 2), pl.ds(left, width)]

    def place(k):
        return crop.at[pl.ds(2 * k, 2)]

    sends = []
    for j in range(units):
        index = units * me + j - base
        for k, ok, target in (
            (1, (index >= 0) & (index < size), index),
            (0, index == -1, 0),
            (2, index == size, size - 1),
        ):
            if j != units - 1 and k == 0:
                continue
            if j != 0 and k == 2:
                continue
            copy = remote(unit(j), place(k), len(sends), k, target)
            far = ok & (target != me)
            sends.append((far, copy))
            pl.when(far)(copy.start)
            if k == 1:
                near = pltpu.make_async_copy(unit(j), place(1), local)

                @pl.when(ok & (target == me))
                def _():
                    near.start()
                    near.wait()

    has_up, has_down = me > 0, me < size - 1
    for ok, peer, src, dst, slot in (
        (has_up, me - 1, ctx.at[pl.ds(0, 2)], c_bot, 3),
        (has_down, me + 1, ctx.at[pl.ds(rows - 2, 2)], c_top, 4),
        (has_up, me - 1, cot.at[pl.ds(0, 1)], g_bot, 5),
        (has_down, me + 1, cot.at[pl.ds(rows - 1, 1)], g_top, 6),
    ):
        copy = remote(src, dst, len(sends), slot, peer)
        sends.append((ok, copy))
        pl.when(ok)(copy.start)

    @pl.when(me == 0)
    def _():
        c_top[...] = jnp.zeros_like(c_top)
        g_top[...] = jnp.zeros_like(g_top)

    @pl.when(me == size - 1)
    def _():
        c_bot[...] = jnp.zeros_like(c_bot)
        g_bot[...] = jnp.zeros_like(g_bot)

    mine = (base + me) // units
    take = remote(place(1), place(1), 0, 1, me)
    pl.when(mine != me)(take.wait_recv)
    for ok, peer, k in ((has_up, me - 1, 2), (has_down, me + 1, 0)):
        copy = remote(place(1), place(k), len(sends), k, peer)
        sends.append((ok, copy))
        pl.when(ok)(copy.start)
    for k in (0, 2):
        remote(place(k), place(k), 0, k, me).wait_recv()
    pl.when(has_up)(remote(c_top, c_top, 0, 4, me).wait_recv)
    pl.when(has_up)(remote(g_top, g_top, 0, 6, me).wait_recv)
    pl.when(has_down)(remote(c_bot, c_bot, 0, 3, me).wait_recv)
    pl.when(has_down)(remote(g_bot, g_bot, 0, 5, me).wait_recv)
    for ok, copy in sends:
        pl.when(ok)(copy.wait_send)


def gather(size, context, cot_context, left, width):
    rows, cols, channels = context.shape
    shapes = [(2, cols, channels)] * 2 + [(1, cols, channels)] * 2 + [(6, width, channels)]
    return pl.pallas_call(
        functools.partial(gather_kernel, size, left, width),
        out_shape=[jax.ShapeDtypeStruct(shape, BF) for shape in shapes],
        in_specs=[pl.BlockSpec(memory_space=pl.ANY)] * 2,
        out_specs=[pl.BlockSpec(memory_space=pltpu.VMEM)] * 5,
        scratch_shapes=[
            pltpu.SemaphoreType.DMA((rows // 2 + 8,)),
            pltpu.SemaphoreType.DMA((7,)),
            pltpu.SemaphoreType.DMA,
        ],
        compiler_params=pltpu.CompilerParams(
            collective_id=0, has_side_effects=True, vmem_limit_bytes=VMEM_LIMIT
        ),
    )(context, cot_context)


def fine_kernel(
    size, lead, crop_ctx, conv_w, bias, proj, blend, blend_t, hr, cot,
    joined, wgrad, parts, crop, upper, acc,
):
    step = pl.program_id(0)
    me = lax.axis_index("rows")
    channels = hr.shape[2]
    cols = hr.shape[1]
    narrow, wide = blend.shape[1], crop_ctx.shape[1]
    chunk = 128

    @pl.when(step == 0)
    def _():
        shifted = []
        for b in range(3):
            total = None
            for a in range(3):
                rows = crop_ctx[pl.ds(a, 4)].reshape(4 * wide, channels)
                term = dot(rows, conv_w[a, b])
                total = term if total is None else total + term
            shifted.append(total.reshape(4, wide, channels))
        for row in range(4):
            pre = bias[...] + sum(
                shifted[b][row, lead + b - 1 : lead + b - 1 + narrow] for b in range(3)
            )
            value = crop_ctx[row + 1, lead : lead + narrow].astype(F32) + pre * sigmoid(pre)
            crop[row] = value.astype(BF)

        @pl.when(me == 0)
        def _():
            crop[0] = crop[1]

        @pl.when(me == size - 1)
        def _():
            crop[3] = crop[2]

        for row in range(4):
            coarse = dot(crop[row], proj[pl.ds(channels, channels)]).astype(BF)
            upper[row] = dot(blend[...], coarse)
        acc[...] = jnp.zeros_like(acc)
        wgrad[...] = jnp.zeros_like(wgrad)

    low = (step + 1) // 2
    start = jnp.where(step % 2 == 0, 9, 1)
    weights = [(2 * k + start).astype(F32) * (1.0 / 16.0) for k in range(4)]

    def body(c, carry):
        at = pl.ds(pl.multiple_of(c * chunk, chunk), chunk)
        lo, hi = upper[low, at], upper[low + 1, at]
        x = hr[:, at].reshape(4 * chunk, channels)
        base = dot(x, proj[pl.ds(0, channels)])
        grads = []
        first = second = None
        for k in range(4):
            v = base[k * chunk : (k + 1) * chunk] + (lo + weights[k] * (hi - lo))
            s = sigmoid(v)
            j = v * s
            joined[k, at] = j.astype(BF)
            g = (cot[k, at].astype(F32) * (s + j * (1.0 - s))).astype(BF)
            grads.append(g)
            g = g.astype(F32)
            part = weights[k] * g
            second = part if second is None else second + part
            rest = g - part
            first = rest if first is None else first + rest
        acc[low, at] += first
        acc[low + 1, at] += second
        wgrad[pl.ds(0, channels)] += t_dot(x, jnp.concatenate(grads, axis=0))
        return carry

    lax.fori_loop(0, cols // chunk, body, 0)

    @pl.when(step == pl.num_programs(0) - 1)
    def _():
        back = [dot(blend_t[...], acc[row].astype(BF)) for row in range(4)]
        top = jnp.where(me == 0, 1.0, 0.0)
        bottom = jnp.where(me == size - 1, 1.0, 0.0)
        back[1] = back[1] + top * back[0]
        back[2] = back[2] + bottom * back[3]
        back = [back[0] * (1.0 - top), back[1], back[2], back[3] * (1.0 - bottom)]
        bottom_w = proj[pl.ds(channels, channels)]
        total = None
        for row in range(4):
            low_back = back[row].astype(BF)
            parts[row] = dot_t(low_back, bottom_w)
            term = t_dot(crop[row], low_back)
            total = term if total is None else total + term
        wgrad[pl.ds(channels, channels)] = total


def fine(size, lead, crop_ctx, conv_weight, conv_bias, proj_weight, hr, cot):
    fine_rows, cols, channels = hr.shape
    narrow = cols // 8
    index = 2 * np.arange(cols) - 7
    lower = index // 16
    frac = ((index - 16 * lower) / 16.0)[:, None]
    column = np.arange(narrow)[None, :]
    left = np.clip(lower, 0, narrow - 1)[:, None]
    right = np.clip(lower + 1, 0, narrow - 1)[:, None]
    blend = (1.0 - frac) * (column == left) + frac * (column == right)
    blend, blend_t = jnp.asarray(blend, BF), jnp.asarray(blend.T, BF)
    whole = lambda shape: pl.BlockSpec(shape, lambda s: (0,) * len(shape))
    tile = pl.BlockSpec((4, cols, channels), lambda s: (s, 0, 0))
    return pl.pallas_call(
        functools.partial(fine_kernel, size, lead),
        grid=(fine_rows // 4,),
        out_shape=[
            jax.ShapeDtypeStruct(hr.shape, BF),
            jax.ShapeDtypeStruct((2 * channels, channels), F32),
            jax.ShapeDtypeStruct((4, narrow, channels), F32),
        ],
        in_specs=[
            whole(crop_ctx.shape),
            whole(conv_weight.shape),
            whole((1, channels)),
            whole(proj_weight.shape),
            whole((cols, narrow)),
            whole((narrow, cols)),
            tile,
            tile,
        ],
        out_specs=[tile, whole((2 * channels, channels)), whole((4, narrow, channels))],
        scratch_shapes=[
            pltpu.VMEM((4, narrow, channels), BF),
            pltpu.VMEM((4, cols, channels), F32),
            pltpu.VMEM((4, cols, channels), F32),
        ],
        compiler_params=pltpu.CompilerParams(vmem_limit_bytes=VMEM_LIMIT),
    )(crop_ctx, conv_weight, conv_bias.reshape(1, -1), proj_weight, blend, blend_t, hr, cot)


def scatter_kernel(
    size, units, parts, ctx, c_top, c_bot, conv_w, bias, out, slope, ext, up, down, got_up, got_down, mine, send, recv, edge,
):
    group, me = enter(size)
    base = 3 * size // 2

    def remote(src, dst, s, r, peer):
        return pltpu.make_async_remote_copy(
            src_ref=src,
            dst_ref=dst,
            send_sem=s,
            recv_sem=r,
            device_id=(group, peer),
            device_id_type=MESH,
        )

    has_up, has_down = me > 0, me < size - 1
    up[...] = parts[0].astype(BF)
    down[...] = parts[3].astype(BF)
    to_up = remote(up, got_down, send.at[0], edge.at[0], me - 1)
    to_down = remote(down, got_up, send.at[1], edge.at[1], me + 1)
    pl.when(has_up)(to_up.start)
    pl.when(has_down)(to_down.start)

    @pl.when(me == 0)
    def _():
        got_up[...] = jnp.zeros_like(got_up)

    @pl.when(me == size - 1)
    def _():
        got_down[...] = jnp.zeros_like(got_down)

    rows, cols, channels = ctx.shape
    ext[pl.ds(0, 2)] = c_top[...]
    ext[pl.ds(2, rows)] = ctx[...]
    ext[pl.ds(rows + 2, 2)] = c_bot[...]
    column = lax.broadcasted_iota(jnp.int32, (cols, channels), 0)

    def forward(p, carry):
        sums = []
        for b in range(3):
            total = None
            for a in range(3):
                term = dot(ext[pl.ds(2 * p + a, 2)].reshape(2 * cols, channels), conv_w[a, b])
                total = term if total is None else total + term
            sums.append(total)
        for k in range(2):
            cut = slice(k * cols, (k + 1) * cols)
            v = bias[...] + jnp.where(column == 0, 0.0, pltpu.roll(sums[0][cut], 1, 0))
            v = v + sums[1][cut]
            v = v + jnp.where(column == cols - 1, 0.0, pltpu.roll(sums[2][cut], cols - 1, 0))
            s = sigmoid(v)
            slope[2 * p + k] = s * (1.0 + v * (1.0 - s))
        return carry

    pairs = (rows + 2) // 2
    lax.fori_loop(0, pairs - 2, forward, 0)

    for s in range(units + 2):
        index = units * me + s - 1 - base

        @pl.when((index < 0) | (index >= size))
        def _():
            out[s] = jnp.zeros_like(out[s])

    pl.when(has_up)(remote(got_up, got_up, send.at[0], edge.at[1], me).wait_recv)
    pl.when(has_down)(remote(got_down, got_down, send.at[0], edge.at[0], me).wait_recv)
    mine[0] = (parts[1] + got_up[...].astype(F32)).astype(BF)
    mine[1] = (parts[2] + got_down[...].astype(F32)).astype(BF)
    number = base + me
    waits = []
    for s in range(units + 2):
        offset = number + 1 - s
        owner = offset // units
        ok = lax.rem(offset, units) == 0
        copy = remote(mine, out.at[s], send.at[2 + s], recv.at[s], owner)
        far = ok & (owner != me) & (owner >= 0) & (owner < size)
        waits.append((far, copy))
        pl.when(far)(copy.start)

        @pl.when(ok & (owner == me))
        def _():
            out[s] = mine[...]

    lax.fori_loop(pairs - 2, pairs, forward, 0)
    for s in range(units + 2):
        index = units * me + s - 1 - base
        here = (index >= 0) & (index < size) & (index != me)
        pl.when(here)(remote(mine, out.at[s], send.at[0], recv.at[s], me).wait_recv)
    for far, copy in waits:
        pl.when(far)(copy.wait_send)
    pl.when(has_up)(to_up.wait_send)
    pl.when(has_down)(to_down.wait_send)


def scatter(size, units, parts, context, c_top, c_bot, conv_weight, conv_bias):
    rows, cols, _ = context.shape
    _, narrow, channels = parts.shape
    row = (narrow, channels)
    return pl.pallas_call(
        functools.partial(scatter_kernel, size, units),
        out_shape=[
            jax.ShapeDtypeStruct((units + 2, 2) + row, BF),
            jax.ShapeDtypeStruct((rows + 2, cols, channels), F32),
        ],
        in_specs=[pl.BlockSpec(memory_space=pltpu.VMEM)] * 6,
        out_specs=[pl.BlockSpec(memory_space=pltpu.VMEM)] * 2,
        scratch_shapes=[pltpu.VMEM((rows + 4, cols, channels), BF)]
        + [pltpu.VMEM(row, BF)] * 4
        + [
            pltpu.VMEM((2,) + row, BF),
            pltpu.SemaphoreType.DMA((units + 4,)),
            pltpu.SemaphoreType.DMA((units + 2,)),
            pltpu.SemaphoreType.DMA((2,)),
        ],
        compiler_params=pltpu.CompilerParams(
            collective_id=1, has_side_effects=True, vmem_limit_bytes=VMEM_LIMIT
        ),
    )(parts, context, c_top, c_bot, conv_weight, conv_bias.reshape(1, -1))


def coarse_kernel(
    left, ctx, c_top, c_bot, cot, g_top, g_bot, crop_grad, conv_w, slope,
    grad, wgrad, bgrad, ext, ext_t, outg, pre_g,
):
    rows, cols, channels = ctx.shape
    narrow = crop_grad.shape[1]
    ext[pl.ds(0, 2)] = c_top[...]
    ext[pl.ds(2, rows)] = ctx[...]
    ext[pl.ds(rows + 2, 2)] = c_bot[...]
    outg[pl.ds(0, 1)] = g_top[...].astype(F32)
    outg[pl.ds(1, rows)] = cot[...].astype(F32)
    outg[pl.ds(rows + 1, 1)] = g_bot[...].astype(F32)
    for r in range(rows + 2):
        outg[r, pl.ds(left, narrow)] += crop_grad[r + 1].astype(F32)
    column = lax.broadcasted_iota(jnp.int32, (cols, channels), 0)

    def later(v):
        return jnp.where(column == 0, 0.0, pltpu.roll(v, 1, 0))

    def sooner(v):
        return jnp.where(column == cols - 1, 0.0, pltpu.roll(v, cols - 1, 0))

    def turn(r, carry):
        ext_t[r] = jnp.transpose(ext[r + 1])
        return carry

    lax.fori_loop(0, rows + 2, turn, 0)
    bgrad[...] = jnp.zeros_like(bgrad)

    def forward(r, carry):
        g = (outg[r] * slope[r]).astype(BF)
        pre_g[1, r] = g
        g = g.astype(F32)
        pre_g[0, r] = sooner(g).astype(BF)
        pre_g[2, r] = later(g).astype(BF)
        own = ((r >= 1) & (r <= rows)).astype(F32)
        bgrad[pl.ds(0, 1)] += own * jnp.sum(g, axis=0, keepdims=True)
        return carry

    lax.fori_loop(0, rows + 2, forward, 0)

    def backward(p, carry):
        sums = []
        for b in range(3):
            total = None
            for a in range(3):
                term = dot_t(
                    pre_g[1, pl.ds(2 * p + 2 - a, 2)].reshape(2 * cols, channels), conv_w[a, b]
                )
                total = term if total is None else total + term
            sums.append(total)
        for k in range(2):
            cut = slice(k * cols, (k + 1) * cols)
            r = 2 * p + k
            grad[r] = outg[r + 1] + (sooner(sums[0][cut]) + sums[1][cut] + later(sums[2][cut]))
        return carry

    lax.fori_loop(0, rows // 2, backward, 0)

    def weights(n, carry):
        a, b = n // 3, n % 3
        total = None
        for i in range(rows):
            term = dot(ext_t[i + a], pre_g[b, i + 1])
            total = term if total is None else total + term
        wgrad[n] = total
        return carry

    lax.fori_loop(0, 9, weights, 0)


def coarse(left, context, halos, cot_context, crop_grad, conv_weight, slope):
    rows, cols, channels = context.shape
    c_top, c_bot, g_top, g_bot = halos
    return pl.pallas_call(
        functools.partial(coarse_kernel, left),
        out_shape=[
            jax.ShapeDtypeStruct((rows, cols, channels), F32),
            jax.ShapeDtypeStruct((9, channels, channels), F32),
            jax.ShapeDtypeStruct((8, channels), F32),
        ],
        in_specs=[pl.BlockSpec(memory_space=pltpu.VMEM)] * 9,
        out_specs=[pl.BlockSpec(memory_space=pltpu.VMEM)] * 3,
        scratch_shapes=[
            pltpu.VMEM((rows + 4, cols, channels), BF),
            pltpu.VMEM((rows + 2, channels, cols), BF),
            pltpu.VMEM((rows + 2, cols, channels), F32),
            pltpu.VMEM((3, rows + 2, cols, channels), BF),
        ],
        compiler_params=pltpu.CompilerParams(vmem_limit_bytes=VMEM_LIMIT),
    )(context, c_top, c_bot, cot_context, g_top, g_bot, crop_grad, conv_weight, slope)


def reduce_kernel(size, conv, proj, bias, out, acc, outgoing, incoming, send, recv, back, load):
    group, me = lax.axis_index("groups"), lax.axis_index("rows")
    total_rows, channels = acc.shape
    half = channels // 2
    bits = [2**k for k in range(size.bit_length() - 1)]
    orders = (bits, bits[:1] + bits[2:] + bits[1:2])
    steps = len(bits)
    n_conv, n_proj, n_bias = conv.shape[0], proj.shape[0], bias.shape[0]
    loads = [
        pltpu.make_async_copy(conv, acc.at[pl.ds(0, n_conv)], load.at[0]),
        pltpu.make_async_copy(proj, acc.at[pl.ds(n_conv, n_proj)], load.at[1]),
        pltpu.make_async_copy(bias, acc.at[pl.ds(n_conv + n_proj, n_bias)], load.at[2]),
    ]
    for copy in loads:
        copy.start()
    used = n_conv + n_proj + n_bias
    acc[pl.ds(used, total_rows - used)] = jnp.zeros((total_rows - used, channels), F32)

    def side(bit):
        return lax.rem(me // bit, 2)

    def partner(bit):
        return me + bit * (1 - 2 * side(bit))

    barrier = pltpu.get_barrier_semaphore()
    for bit in bits:
        pl.semaphore_signal(barrier, inc=1, device_id=(group, partner(bit)), device_id_type=MESH)
    pl.semaphore_wait(barrier, steps)
    for copy in loads:
        copy.wait()

    def remote(src, dst, s, r, bit):
        return pltpu.make_async_remote_copy(
            src_ref=src,
            dst_ref=dst,
            send_sem=s,
            recv_sem=r,
            device_id=(group, partner(bit)),
            device_id_type=MESH,
        )

    def rows_at(start, count):
        return pl.ds(pl.multiple_of(start, 16), count)

    low = [0, 0]
    kept = [[], []]
    copies = []
    pending = [None, None]
    for step in range(steps + 1):
        for h in range(2):
            lanes = pl.ds(h * half, half)
            if step > 0:
                count = total_rows >> step
                pending[h].wait_recv()
                got = incoming[pl.ds(total_rows - 2 * count, count), lanes]
                acc[rows_at(low[h], count), lanes] += got.astype(F32)
            if step < steps:
                bit = orders[h][step]
                count = total_rows >> (step + 1)
                mine = low[h] + side(bit) * count
                other = low[h] + (1 - side(bit)) * count
                there = rows_at(other, count)
                outgoing[there, lanes] = acc[there, lanes].astype(BF)
                copy = remote(
                    outgoing.at[there, lanes],
                    incoming.at[pl.ds(total_rows - 2 * count, count), lanes],
                    send.at[h, step],
                    recv.at[h, step],
                    bit,
                )
                copy.start()
                copies.append(copy)
                pending[h] = copy
                low[h] = mine
                kept[h].append(mine)
            else:
                here = rows_at(low[h], total_rows >> steps)
                out[here, lanes] = acc[here, lanes].astype(BF)
                bit = orders[h][steps - 1]
                copy = remote(
                    out.at[here, lanes],
                    out.at[here, lanes],
                    send.at[h, steps],
                    back.at[h, steps - 1],
                    bit,
                )
                copy.start()
                copies.append(copy)
                pending[h] = copy
    for step in reversed(range(steps)):
        for h in range(2):
            lanes = pl.ds(h * half, half)
            pending[h].wait_recv()
            if step > 0:
                here = rows_at(kept[h][step - 1], total_rows >> step)
                copy = remote(
                    out.at[here, lanes],
                    out.at[here, lanes],
                    send.at[h, 2 * steps - step],
                    back.at[h, step - 1],
                    orders[h][step - 1],
                )
                copy.start()
                copies.append(copy)
                pending[h] = copy
    for copy in copies:
        copy.wait_send()


def reduce_sums(size, conv, proj, bias):
    channels = conv.shape[1]
    rows = conv.shape[0] + proj.shape[0] + bias.shape[0]
    rows = -(-rows // (16 * size)) * 16 * size
    steps = size.bit_length() - 1
    return pl.pallas_call(
        functools.partial(reduce_kernel, size),
        out_shape=jax.ShapeDtypeStruct((rows, channels), BF),
        in_specs=[pl.BlockSpec(memory_space=pl.ANY)] * 3,
        out_specs=pl.BlockSpec(memory_space=pltpu.VMEM),
        scratch_shapes=[
            pltpu.VMEM((rows, channels), F32),
            pltpu.VMEM((rows, channels), BF),
            pltpu.VMEM((rows, channels), BF),
            pltpu.SemaphoreType.DMA((2, 2 * steps)),
            pltpu.SemaphoreType.DMA((2, steps)),
            pltpu.SemaphoreType.DMA((2, steps)),
            pltpu.SemaphoreType.DMA((3,)),
        ],
        compiler_params=pltpu.CompilerParams(
            collective_id=2, has_side_effects=True, vmem_limit_bytes=VMEM_LIMIT
        ),
    )(conv, proj, bias)


def widen_kernel(sums, conv, proj, bias):
    n_conv, n_proj = conv.shape[0], proj.shape[0]
    step = 256

    def body(n, carry):
        at = pl.ds(pl.multiple_of(n * step, step), step)
        conv[at] = sums[at].astype(F32)
        return carry

    lax.fori_loop(0, n_conv // step, body, 0)
    proj[...] = sums[pl.ds(n_conv, n_proj)].astype(F32)
    bias[...] = sums[pl.ds(n_conv + n_proj, 16)].astype(F32)[:1]


def widen(sums):
    channels = sums.shape[1]
    return pl.pallas_call(
        widen_kernel,
        out_shape=[jax.ShapeDtypeStruct((n, channels), F32) for n in (9 * channels, 2 * channels, 1)],
        in_specs=[pl.BlockSpec(memory_space=pltpu.VMEM)],
        out_specs=[pl.BlockSpec(memory_space=pltpu.VMEM)] * 3,
        compiler_params=pltpu.CompilerParams(vmem_limit_bytes=VMEM_LIMIT),
    )(sums)


def per_device(size, context, conv_weight, conv_bias, hr_features, proj_weight, cot_joined,
               cot_context):
    rows, cols, channels = context.shape
    narrow = hr_features.shape[1] // 8
    left = (cols - narrow) // 2
    lead = 16
    *halos, crop_ctx = gather(size, context, cot_context, left - lead, narrow + 2 * lead)
    joined, proj_grad, parts = fine(
        size, lead, crop_ctx, conv_weight, conv_bias, proj_weight, hr_features, cot_joined
    )
    crop_grad, slope = scatter(
        size, rows // 2, parts, context, *halos[:2], conv_weight, conv_bias
    )
    crop_grad = crop_grad.reshape(-1, narrow, channels)
    grad, conv_grad, bias_grad = coarse(
        left, context, halos, cot_context, crop_grad, conv_weight, slope
    )
    conv_sum, proj_sum, bias_sum = widen(
        reduce_sums(size, conv_grad.reshape(-1, channels), proj_grad, bias_grad)
    )
    return (
        joined,
        grad,
        conv_sum.reshape(3, 3, channels, channels),
        bias_sum.reshape(-1),
        proj_sum,
    )


def solution(mesh):
    tile = P(("groups", "rows"), None, None)
    return jax.shard_map(
        functools.partial(per_device, mesh.shape["rows"]),
        mesh=mesh,
        in_specs=(tile, P(), P(), tile, P(), tile, tile),
        out_specs=(tile, tile, P("groups", None, None, None), P("groups"), P("groups", None)),
        check_vma=False,
    )
```

```python
import functools

import jax
import jax.numpy as jnp
import numpy as np
from jax import lax
from jax.experimental import pallas as pl
from jax.experimental.pallas import tpu as pltpu
from jax.sharding import PartitionSpec as P

MESH = pl.DeviceIdType.MESH
BF = jnp.bfloat16
F32 = jnp.float32
VMEM_LIMIT = 56 * 1024 * 1024


def dot(lhs, rhs):
    return jnp.dot(lhs, rhs, preferred_element_type=F32)


def dot_t(lhs, rhs):
    return lax.dot_general(lhs, rhs, (((1,), (1,)), ((), ())), preferred_element_type=F32)


def t_dot(lhs, rhs):
    return lax.dot_general(lhs, rhs, (((0,), (0,)), ((), ())), preferred_element_type=F32)


def sigmoid(values):
    return 0.5 * jnp.tanh(0.5 * values) + 0.5


def enter(size):
    group, me = lax.axis_index("groups"), lax.axis_index("rows")
    barrier = pltpu.get_barrier_semaphore()

    def greet(step, carry):
        peer = lax.rem(me + step, size)
        pl.semaphore_signal(barrier, inc=1, device_id=(group, peer), device_id_type=MESH)
        return carry

    lax.fori_loop(1, size, greet, 0)
    pl.semaphore_wait(barrier, size - 1)
    return group, me


def gather_kernel(size, left, width, ctx, crop, send, recv, local):
    group, me = enter(size)
    rows = ctx.shape[0]
    units = rows // 2
    base = 3 * size // 2

    def remote(src, dst, number, slot, peer):
        return pltpu.make_async_remote_copy(
            src_ref=src,
            dst_ref=dst,
            send_sem=send.at[number],
            recv_sem=recv.at[slot],
            device_id=(group, peer),
            device_id_type=MESH,
        )

    def unit(j):
        return ctx.at[pl.ds(2 * j, 2), pl.ds(left, width)]

    def place(k):
        return crop.at[pl.ds(2 * k, 2)]

    sends = []
    for j in range(units):
        index = units * me + j - base
        for k, ok, target in (
            (1, (index >= 0) & (index < size), index),
            (0, index == -1, 0),
            (2, index == size, size - 1),
        ):
            if j != units - 1 and k == 0:
                continue
            if j != 0 and k == 2:
                continue
            copy = remote(unit(j), place(k), len(sends), k, target)
            far = ok & (target != me)
            sends.append((far, copy))
            pl.when(far)(copy.start)
            if k == 1:
                near = pltpu.make_async_copy(unit(j), place(1), local)

                @pl.when(ok & (target == me))
                def _():
                    near.start()
                    near.wait()

    has_up, has_down = me > 0, me < size - 1
    mine = (base + me) // units
    take = remote(place(1), place(1), 0, 1, me)
    pl.when(mine != me)(take.wait_recv)
    for ok, peer, k in ((has_up, me - 1, 2), (has_down, me + 1, 0)):
        copy = remote(place(1), place(k), len(sends), k, peer)
        sends.append((ok, copy))
        pl.when(ok)(copy.start)
    for k in (0, 2):
        remote(place(k), place(k), 0, k, me).wait_recv()
    for ok, copy in sends:
        pl.when(ok)(copy.wait_send)


def gather(size, context, left, width):
    rows, _, channels = context.shape
    return pl.pallas_call(
        functools.partial(gather_kernel, size, left, width),
        out_shape=jax.ShapeDtypeStruct((6, width, channels), BF),
        in_specs=[pl.BlockSpec(memory_space=pl.ANY)],
        out_specs=pl.BlockSpec(memory_space=pltpu.VMEM),
        scratch_shapes=[
            pltpu.SemaphoreType.DMA((rows // 2 + 8,)),
            pltpu.SemaphoreType.DMA((3,)),
            pltpu.SemaphoreType.DMA,
        ],
        compiler_params=pltpu.CompilerParams(
            collective_id=0, has_side_effects=True, vmem_limit_bytes=VMEM_LIMIT
        ),
    )(context)


def fine_kernel(
    size, lead, crop_ctx, conv_w, bias, proj, blend, blend_t, hr, cot,
    joined, wgrad, parts, crop, upper, acc,
):
    step = pl.program_id(0)
    me = lax.axis_index("rows")
    channels = hr.shape[2]
    cols = hr.shape[1]
    narrow, wide = blend.shape[1], crop_ctx.shape[1]
    chunk = 128

    @pl.when(step == 0)
    def _():
        shifted = []
        for b in range(3):
            total = None
            for a in range(3):
                rows = crop_ctx[pl.ds(a, 4)].reshape(4 * wide, channels)
                term = dot(rows, conv_w[a, b])
                total = term if total is None else total + term
            shifted.append(total.reshape(4, wide, channels))
        for row in range(4):
            pre = bias[...] + sum(
                shifted[b][row, lead + b - 1 : lead + b - 1 + narrow] for b in range(3)
            )
            value = crop_ctx[row + 1, lead : lead + narrow].astype(F32) + pre * sigmoid(pre)
            crop[row] = value.astype(BF)

        @pl.when(me == 0)
        def _():
            crop[0] = crop[1]

        @pl.when(me == size - 1)
        def _():
            crop[3] = crop[2]

        for row in range(4):
            coarse = dot(crop[row], proj[pl.ds(channels, channels)]).astype(BF)
            upper[row] = dot(blend[...], coarse)
        acc[...] = jnp.zeros_like(acc)
        wgrad[...] = jnp.zeros_like(wgrad)

    low = (step + 1) // 2
    start = jnp.where(step % 2 == 0, 9, 1)
    weights = [(2 * k + start).astype(F32) * (1.0 / 16.0) for k in range(4)]

    def body(c, carry):
        at = pl.ds(pl.multiple_of(c * chunk, chunk), chunk)
        lo, hi = upper[low, at], upper[low + 1, at]
        x = hr[:, at].reshape(4 * chunk, channels)
        base = dot(x, proj[pl.ds(0, channels)])
        grads = []
        first = second = None
        for k in range(4):
            v = base[k * chunk : (k + 1) * chunk] + (lo + weights[k] * (hi - lo))
            s = sigmoid(v)
            j = v * s
            joined[k, at] = j.astype(BF)
            g = (cot[k, at].astype(F32) * (s + j * (1.0 - s))).astype(BF)
            grads.append(g)
            g = g.astype(F32)
            part = weights[k] * g
            second = part if second is None else second + part
            rest = g - part
            first = rest if first is None else first + rest
        acc[low, at] += first
        acc[low + 1, at] += second
        wgrad[pl.ds(0, channels)] += t_dot(x, jnp.concatenate(grads, axis=0))
        return carry

    lax.fori_loop(0, cols // chunk, body, 0)

    @pl.when(step == pl.num_programs(0) - 1)
    def _():
        back = [dot(blend_t[...], acc[row].astype(BF)) for row in range(4)]
        top = jnp.where(me == 0, 1.0, 0.0)
        bottom = jnp.where(me == size - 1, 1.0, 0.0)
        back[1] = back[1] + top * back[0]
        back[2] = back[2] + bottom * back[3]
        back = [back[0] * (1.0 - top), back[1], back[2], back[3] * (1.0 - bottom)]
        bottom_w = proj[pl.ds(channels, channels)]
        total = None
        for row in range(4):
            low_back = back[row].astype(BF)
            parts[row] = dot_t(low_back, bottom_w)
            term = t_dot(crop[row], low_back)
            total = term if total is None else total + term
        wgrad[pl.ds(channels, channels)] = total


def fine(size, lead, crop_ctx, conv_weight, conv_bias, proj_weight, hr, cot):
    fine_rows, cols, channels = hr.shape
    narrow = cols // 8
    index = 2 * np.arange(cols) - 7
    lower = index // 16
    frac = ((index - 16 * lower) / 16.0)[:, None]
    column = np.arange(narrow)[None, :]
    left = np.clip(lower, 0, narrow - 1)[:, None]
    right = np.clip(lower + 1, 0, narrow - 1)[:, None]
    blend = (1.0 - frac) * (column == left) + frac * (column == right)
    blend, blend_t = jnp.asarray(blend, BF), jnp.asarray(blend.T, BF)
    whole = lambda shape: pl.BlockSpec(shape, lambda s: (0,) * len(shape))
    tile = pl.BlockSpec((4, cols, channels), lambda s: (s, 0, 0))
    return pl.pallas_call(
        functools.partial(fine_kernel, size, lead),
        grid=(fine_rows // 4,),
        out_shape=[
            jax.ShapeDtypeStruct(hr.shape, BF),
            jax.ShapeDtypeStruct((2 * channels, channels), F32),
            jax.ShapeDtypeStruct((4, narrow, channels), F32),
        ],
        in_specs=[
            whole(crop_ctx.shape),
            whole(conv_weight.shape),
            whole((1, channels)),
            whole(proj_weight.shape),
            whole((cols, narrow)),
            whole((narrow, cols)),
            tile,
            tile,
        ],
        out_specs=[tile, whole((2 * channels, channels)), whole((4, narrow, channels))],
        scratch_shapes=[
            pltpu.VMEM((4, narrow, channels), BF),
            pltpu.VMEM((4, cols, channels), F32),
            pltpu.VMEM((4, cols, channels), F32),
        ],
        compiler_params=pltpu.CompilerParams(vmem_limit_bytes=VMEM_LIMIT),
    )(crop_ctx, conv_weight, conv_bias.reshape(1, -1), proj_weight, blend, blend_t, hr, cot)


def scatter_kernel(
    size, units, parts, ctx, cot, conv_w, bias, out, slope, g_top, g_bot,
    ext, up, down, got_up, got_down, mine, send, recv, edge, h_send, h_recv,
):
    group, me = enter(size)
    base = 3 * size // 2

    def remote(src, dst, s, r, peer):
        return pltpu.make_async_remote_copy(
            src_ref=src,
            dst_ref=dst,
            send_sem=s,
            recv_sem=r,
            device_id=(group, peer),
            device_id_type=MESH,
        )

    has_up, has_down = me > 0, me < size - 1
    up[...] = parts[0].astype(BF)
    down[...] = parts[3].astype(BF)
    to_up = remote(up, got_down, send.at[0], edge.at[0], me - 1)
    to_down = remote(down, got_up, send.at[1], edge.at[1], me + 1)
    pl.when(has_up)(to_up.start)
    pl.when(has_down)(to_down.start)

    @pl.when(me == 0)
    def _():
        got_up[...] = jnp.zeros_like(got_up)

    @pl.when(me == size - 1)
    def _():
        got_down[...] = jnp.zeros_like(got_down)

    rows, cols, channels = ctx.shape
    above, below = ext.at[pl.ds(0, 2)], ext.at[pl.ds(rows + 2, 2)]
    halos = []
    for n, (ok, peer, src, dst) in enumerate((
        (has_up, me - 1, ctx.at[pl.ds(0, 2)], below),
        (has_down, me + 1, ctx.at[pl.ds(rows - 2, 2)], above),
        (has_up, me - 1, cot.at[pl.ds(0, 1)], g_bot),
        (has_down, me + 1, cot.at[pl.ds(rows - 1, 1)], g_top),
    )):
        copy = remote(src, dst, h_send.at[n], h_recv.at[n], peer)
        halos.append((ok, copy))
        pl.when(ok)(copy.start)

    @pl.when(me == 0)
    def _():
        ext[pl.ds(0, 2)] = jnp.zeros((2, cols, channels), BF)
        g_top[...] = jnp.zeros_like(g_top)

    @pl.when(me == size - 1)
    def _():
        ext[pl.ds(rows + 2, 2)] = jnp.zeros((2, cols, channels), BF)
        g_bot[...] = jnp.zeros_like(g_bot)

    ext[pl.ds(2, rows)] = ctx[...]
    column = lax.broadcasted_iota(jnp.int32, (cols, channels), 0)

    def forward(p, carry):
        sums = []
        for b in range(3):
            total = None
            for a in range(3):
                term = dot(ext[pl.ds(2 * p + a, 2)].reshape(2 * cols, channels), conv_w[a, b])
                total = term if total is None else total + term
            sums.append(total)
        for k in range(2):
            cut = slice(k * cols, (k + 1) * cols)
            v = bias[...] + jnp.where(column == 0, 0.0, pltpu.roll(sums[0][cut], 1, 0))
            v = v + sums[1][cut]
            v = v + jnp.where(column == cols - 1, 0.0, pltpu.roll(sums[2][cut], cols - 1, 0))
            s = sigmoid(v)
            slope[2 * p + k] = s * (1.0 + v * (1.0 - s))
        return carry

    pairs = (rows + 2) // 2
    lax.fori_loop(1, pairs - 1, forward, 0)

    for s in range(units + 2):
        index = units * me + s - 1 - base

        @pl.when((index < 0) | (index >= size))
        def _():
            out[s] = jnp.zeros_like(out[s])

    pl.when(has_up)(remote(got_up, got_up, send.at[0], edge.at[1], me).wait_recv)
    pl.when(has_down)(remote(got_down, got_down, send.at[0], edge.at[0], me).wait_recv)
    mine[0] = (parts[1] + got_up[...].astype(F32)).astype(BF)
    mine[1] = (parts[2] + got_down[...].astype(F32)).astype(BF)
    number = base + me
    waits = []
    for s in range(units + 2):
        offset = number + 1 - s
        owner = offset // units
        ok = lax.rem(offset, units) == 0
        copy = remote(mine, out.at[s], send.at[2 + s], recv.at[s], owner)
        far = ok & (owner != me) & (owner >= 0) & (owner < size)
        waits.append((far, copy))
        pl.when(far)(copy.start)

        @pl.when(ok & (owner == me))
        def _():
            out[s] = mine[...]

    for n, (ok, dst) in enumerate(
        ((has_down, below), (has_up, above), (has_down, g_bot), (has_up, g_top))
    ):
        pl.when(ok)(remote(dst, dst, h_send.at[n], h_recv.at[n], me).wait_recv)
    lax.fori_loop(0, 2, lambda n, carry: forward(n * (pairs - 1), carry), 0)
    for ok, copy in halos:
        pl.when(ok)(copy.wait_send)
    for s in range(units + 2):
        index = units * me + s - 1 - base
        here = (index >= 0) & (index < size) & (index != me)
        pl.when(here)(remote(mine, out.at[s], send.at[0], recv.at[s], me).wait_recv)
    for far, copy in waits:
        pl.when(far)(copy.wait_send)
    pl.when(has_up)(to_up.wait_send)
    pl.when(has_down)(to_down.wait_send)


def scatter(size, units, parts, context, cot, conv_weight, conv_bias):
    rows, cols, _ = context.shape
    _, narrow, channels = parts.shape
    row = (narrow, channels)
    return pl.pallas_call(
        functools.partial(scatter_kernel, size, units),
        out_shape=[
            jax.ShapeDtypeStruct((units + 2, 2) + row, BF),
            jax.ShapeDtypeStruct((rows + 2, cols, channels), F32),
            jax.ShapeDtypeStruct((1, cols, channels), BF),
            jax.ShapeDtypeStruct((1, cols, channels), BF),
            jax.ShapeDtypeStruct((rows + 4, cols, channels), BF),
        ],
        in_specs=[pl.BlockSpec(memory_space=pltpu.VMEM)] * 5,
        out_specs=[pl.BlockSpec(memory_space=pltpu.VMEM)] * 5,
        scratch_shapes=[pltpu.VMEM(row, BF)] * 4
        + [
            pltpu.VMEM((2,) + row, BF),
            pltpu.SemaphoreType.DMA((units + 4,)),
            pltpu.SemaphoreType.DMA((units + 2,)),
            pltpu.SemaphoreType.DMA((2,)),
            pltpu.SemaphoreType.DMA((4,)),
            pltpu.SemaphoreType.DMA((4,)),
        ],
        compiler_params=pltpu.CompilerParams(
            collective_id=1, has_side_effects=True, vmem_limit_bytes=VMEM_LIMIT
        ),
    )(parts, context, cot, conv_weight, conv_bias.reshape(1, -1))


def coarse_kernel(
    left, ext, cot, g_top, g_bot, crop_grad, conv_w, slope,
    grad, wgrad, bgrad, ext_t, outg, pre_g,
):
    rows, cols, channels = cot.shape
    narrow = crop_grad.shape[1]
    outg[pl.ds(0, 1)] = g_top[...].astype(F32)
    outg[pl.ds(1, rows)] = cot[...].astype(F32)
    outg[pl.ds(rows + 1, 1)] = g_bot[...].astype(F32)
    for r in range(rows + 2):
        outg[r, pl.ds(left, narrow)] += crop_grad[r + 1].astype(F32)
    column = lax.broadcasted_iota(jnp.int32, (cols, channels), 0)

    def later(v):
        return jnp.where(column == 0, 0.0, pltpu.roll(v, 1, 0))

    def sooner(v):
        return jnp.where(column == cols - 1, 0.0, pltpu.roll(v, cols - 1, 0))

    def turn(r, carry):
        ext_t[r] = jnp.transpose(ext[r + 1])
        return carry

    lax.fori_loop(0, rows + 2, turn, 0)
    bgrad[...] = jnp.zeros_like(bgrad)

    def forward(r, carry):
        g = (outg[r] * slope[r]).astype(BF)
        pre_g[1, r] = g
        g = g.astype(F32)
        pre_g[0, r] = sooner(g).astype(BF)
        pre_g[2, r] = later(g).astype(BF)
        own = ((r >= 1) & (r <= rows)).astype(F32)
        bgrad[pl.ds(0, 1)] += own * jnp.sum(g, axis=0, keepdims=True)
        return carry

    lax.fori_loop(0, rows + 2, forward, 0)

    def backward(p, carry):
        sums = []
        for b in range(3):
            total = None
            for a in range(3):
                term = dot_t(
                    pre_g[1, pl.ds(2 * p + 2 - a, 2)].reshape(2 * cols, channels), conv_w[a, b]
                )
                total = term if total is None else total + term
            sums.append(total)
        for k in range(2):
            cut = slice(k * cols, (k + 1) * cols)
            r = 2 * p + k
            grad[r] = outg[r + 1] + (sooner(sums[0][cut]) + sums[1][cut] + later(sums[2][cut]))
        return carry

    lax.fori_loop(0, rows // 2, backward, 0)

    def weights(n, carry):
        a, b = n // 3, n % 3
        total = None
        for i in range(rows):
            term = dot(ext_t[i + a], pre_g[b, i + 1])
            total = term if total is None else total + term
        wgrad[n] = total
        return carry

    lax.fori_loop(0, 9, weights, 0)


def coarse(left, ext, edges, cot_context, crop_grad, conv_weight, slope):
    rows, cols, channels = cot_context.shape
    g_top, g_bot = edges
    return pl.pallas_call(
        functools.partial(coarse_kernel, left),
        out_shape=[
            jax.ShapeDtypeStruct((rows, cols, channels), F32),
            jax.ShapeDtypeStruct((9, channels, channels), F32),
            jax.ShapeDtypeStruct((8, channels), F32),
        ],
        in_specs=[pl.BlockSpec(memory_space=pltpu.VMEM)] * 7,
        out_specs=[pl.BlockSpec(memory_space=pltpu.VMEM)] * 3,
        scratch_shapes=[
            pltpu.VMEM((rows + 2, channels, cols), BF),
            pltpu.VMEM((rows + 2, cols, channels), F32),
            pltpu.VMEM((3, rows + 2, cols, channels), BF),
        ],
        compiler_params=pltpu.CompilerParams(vmem_limit_bytes=VMEM_LIMIT),
    )(ext, cot_context, g_top, g_bot, crop_grad, conv_weight, slope)


def reduce_kernel(size, conv, proj, bias, out, acc, outgoing, incoming, send, recv, back, load):
    group, me = lax.axis_index("groups"), lax.axis_index("rows")
    total_rows, channels = acc.shape
    half = channels // 2
    bits = [2**k for k in range(size.bit_length() - 1)]
    orders = (bits, bits[:1] + bits[2:] + bits[1:2])
    steps = len(bits)
    n_conv, n_proj, n_bias = conv.shape[0], proj.shape[0], bias.shape[0]
    loads = [
        pltpu.make_async_copy(conv, acc.at[pl.ds(0, n_conv)], load.at[0]),
        pltpu.make_async_copy(proj, acc.at[pl.ds(n_conv, n_proj)], load.at[1]),
        pltpu.make_async_copy(bias, acc.at[pl.ds(n_conv + n_proj, n_bias)], load.at[2]),
    ]
    for copy in loads:
        copy.start()
    used = n_conv + n_proj + n_bias
    acc[pl.ds(used, total_rows - used)] = jnp.zeros((total_rows - used, channels), F32)

    def side(bit):
        return lax.rem(me // bit, 2)

    def partner(bit):
        return me + bit * (1 - 2 * side(bit))

    barrier = pltpu.get_barrier_semaphore()
    for bit in bits:
        pl.semaphore_signal(barrier, inc=1, device_id=(group, partner(bit)), device_id_type=MESH)
    pl.semaphore_wait(barrier, steps)
    for copy in loads:
        copy.wait()

    def remote(src, dst, s, r, bit):
        return pltpu.make_async_remote_copy(
            src_ref=src,
            dst_ref=dst,
            send_sem=s,
            recv_sem=r,
            device_id=(group, partner(bit)),
            device_id_type=MESH,
        )

    def rows_at(start, count):
        return pl.ds(pl.multiple_of(start, 16), count)

    low = [0, 0]
    kept = [[], []]
    copies = []
    pending = [None, None]
    for step in range(steps + 1):
        for h in range(2):
            lanes = pl.ds(h * half, half)
            if step > 0:
                count = total_rows >> step
                pending[h].wait_recv()
                got = incoming[pl.ds(total_rows - 2 * count, count), lanes]
                acc[rows_at(low[h], count), lanes] += got.astype(F32)
            if step < steps:
                bit = orders[h][step]
                count = total_rows >> (step + 1)
                mine = low[h] + side(bit) * count
                other = low[h] + (1 - side(bit)) * count
                there = rows_at(other, count)
                outgoing[there, lanes] = acc[there, lanes].astype(BF)
                copy = remote(
                    outgoing.at[there, lanes],
                    incoming.at[pl.ds(total_rows - 2 * count, count), lanes],
                    send.at[h, step],
                    recv.at[h, step],
                    bit,
                )
                copy.start()
                copies.append(copy)
                pending[h] = copy
                low[h] = mine
                kept[h].append(mine)
            else:
                here = rows_at(low[h], total_rows >> steps)
                out[here, lanes] = acc[here, lanes].astype(BF)
                bit = orders[h][steps - 1]
                copy = remote(
                    out.at[here, lanes],
                    out.at[here, lanes],
                    send.at[h, steps],
                    back.at[h, steps - 1],
                    bit,
                )
                copy.start()
                copies.append(copy)
                pending[h] = copy
    for step in reversed(range(steps)):
        for h in range(2):
            lanes = pl.ds(h * half, half)
            pending[h].wait_recv()
            if step > 0:
                here = rows_at(kept[h][step - 1], total_rows >> step)
                copy = remote(
                    out.at[here, lanes],
                    out.at[here, lanes],
                    send.at[h, 2 * steps - step],
                    back.at[h, step - 1],
                    orders[h][step - 1],
                )
                copy.start()
                copies.append(copy)
                pending[h] = copy
    for copy in copies:
        copy.wait_send()


def reduce_sums(size, conv, proj, bias):
    channels = conv.shape[1]
    rows = conv.shape[0] + proj.shape[0] + bias.shape[0]
    rows = -(-rows // (16 * size)) * 16 * size
    steps = size.bit_length() - 1
    return pl.pallas_call(
        functools.partial(reduce_kernel, size),
        out_shape=jax.ShapeDtypeStruct((rows, channels), BF),
        in_specs=[pl.BlockSpec(memory_space=pl.ANY)] * 3,
        out_specs=pl.BlockSpec(memory_space=pltpu.VMEM),
        scratch_shapes=[
            pltpu.VMEM((rows, channels), F32),
            pltpu.VMEM((rows, channels), BF),
            pltpu.VMEM((rows, channels), BF),
            pltpu.SemaphoreType.DMA((2, 2 * steps)),
            pltpu.SemaphoreType.DMA((2, steps)),
            pltpu.SemaphoreType.DMA((2, steps)),
            pltpu.SemaphoreType.DMA((3,)),
        ],
        compiler_params=pltpu.CompilerParams(
            collective_id=2, has_side_effects=True, vmem_limit_bytes=VMEM_LIMIT
        ),
    )(conv, proj, bias)


def widen_kernel(sums, conv, proj, bias):
    n_conv, n_proj = conv.shape[0], proj.shape[0]
    step = 256

    def body(n, carry):
        at = pl.ds(pl.multiple_of(n * step, step), step)
        conv[at] = sums[at].astype(F32)
        return carry

    lax.fori_loop(0, n_conv // step, body, 0)
    proj[...] = sums[pl.ds(n_conv, n_proj)].astype(F32)
    bias[...] = sums[pl.ds(n_conv + n_proj, 16)].astype(F32)[:1]


def widen(sums):
    channels = sums.shape[1]
    return pl.pallas_call(
        widen_kernel,
        out_shape=[jax.ShapeDtypeStruct((n, channels), F32) for n in (9 * channels, 2 * channels, 1)],
        in_specs=[pl.BlockSpec(memory_space=pltpu.VMEM)],
        out_specs=[pl.BlockSpec(memory_space=pltpu.VMEM)] * 3,
        compiler_params=pltpu.CompilerParams(vmem_limit_bytes=VMEM_LIMIT),
    )(sums)


def per_device(size, context, conv_weight, conv_bias, hr_features, proj_weight, cot_joined,
               cot_context):
    rows, cols, channels = context.shape
    narrow = hr_features.shape[1] // 8
    left = (cols - narrow) // 2
    lead = 16
    crop_ctx = gather(size, context, left - lead, narrow + 2 * lead)
    joined, proj_grad, parts = fine(
        size, lead, crop_ctx, conv_weight, conv_bias, proj_weight, hr_features, cot_joined
    )
    crop_grad, slope, *edges, ext = scatter(
        size, rows // 2, parts, context, cot_context, conv_weight, conv_bias
    )
    crop_grad = crop_grad.reshape(-1, narrow, channels)
    grad, conv_grad, bias_grad = coarse(
        left, ext, edges, cot_context, crop_grad, conv_weight, slope
    )
    conv_sum, proj_sum, bias_sum = widen(
        reduce_sums(size, conv_grad.reshape(-1, channels), proj_grad, bias_grad)
    )
    return (
        joined,
        grad,
        conv_sum.reshape(3, 3, channels, channels),
        bias_sum.reshape(-1),
        proj_sum,
    )


def solution(mesh):
    tile = P(("groups", "rows"), None, None)
    return jax.shard_map(
        functools.partial(per_device, mesh.shape["rows"]),
        mesh=mesh,
        in_specs=(tile, P(), P(), tile, P(), tile, tile),
        out_specs=(tile, tile, P("groups", None, None, None), P("groups"), P("groups", None)),
        check_vma=False,
    )
```

```python
import functools

import jax
import jax.numpy as jnp
import numpy as np
from jax import lax
from jax.experimental import pallas as pl
from jax.experimental.pallas import tpu as pltpu
from jax.sharding import PartitionSpec as P

MESH = pl.DeviceIdType.MESH
BF = jnp.bfloat16
F32 = jnp.float32
VMEM_LIMIT = 56 * 1024 * 1024


def dot(lhs, rhs):
    return jnp.dot(lhs, rhs, preferred_element_type=F32)


def dot_t(lhs, rhs):
    return lax.dot_general(lhs, rhs, (((1,), (1,)), ((), ())), preferred_element_type=F32)


def t_dot(lhs, rhs):
    return lax.dot_general(lhs, rhs, (((0,), (0,)), ((), ())), preferred_element_type=F32)


def sigmoid(values):
    return 0.5 * jnp.tanh(0.5 * values) + 0.5


def enter(size):
    group, me = lax.axis_index("groups"), lax.axis_index("rows")
    barrier = pltpu.get_barrier_semaphore()

    def greet(step, carry):
        peer = lax.rem(me + step, size)
        pl.semaphore_signal(barrier, inc=1, device_id=(group, peer), device_id_type=MESH)
        return carry

    lax.fori_loop(1, size, greet, 0)
    pl.semaphore_wait(barrier, size - 1)
    return group, me


def gather_kernel(size, left, width, ctx, cot, c_top, c_bot, g_top, g_bot, crop, send, recv, local):
    group, me = enter(size)
    rows = ctx.shape[0]
    units = rows // 2
    base = 3 * size // 2

    def remote(src, dst, number, slot, peer):
        return pltpu.make_async_remote_copy(
            src_ref=src,
            dst_ref=dst,
            send_sem=send.at[number],
            recv_sem=recv.at[slot],
            device_id=(group, peer),
            device_id_type=MESH,
        )

    def unit(j):
        return ctx.at[pl.ds(2 * j, 2), pl.ds(left, width)]

    def place(k):
        return crop.at[pl.ds(2 * k, 2)]

    sends = []
    for j in range(units):
        index = units * me + j - base
        for k, ok, target in (
            (1, (index >= 0) & (index < size), index),
            (0, index == -1, 0),
            (2, index == size, size - 1),
        ):
            if j != units - 1 and k == 0:
                continue
            if j != 0 and k == 2:
                continue
            copy = remote(unit(j), place(k), len(sends), k, target)
            far = ok & (target != me)
            sends.append((far, copy))
            pl.when(far)(copy.start)
            if k == 1:
                near = pltpu.make_async_copy(unit(j), place(1), local)

                @pl.when(ok & (target == me))
                def _():
                    near.start()
                    near.wait()

    has_up, has_down = me > 0, me < size - 1
    for ok, peer, src, dst, slot in (
        (has_up, me - 1, ctx.at[pl.ds(0, 2)], c_bot, 3),
        (has_down, me + 1, ctx.at[pl.ds(rows - 2, 2)], c_top, 4),
        (has_up, me - 1, cot.at[pl.ds(0, 1)], g_bot, 5),
        (has_down, me + 1, cot.at[pl.ds(rows - 1, 1)], g_top, 6),
    ):
        copy = remote(src, dst, len(sends), slot, peer)
        sends.append((ok, copy))
        pl.when(ok)(copy.start)

    @pl.when(me == 0)
    def _():
        c_top[...] = jnp.zeros_like(c_top)
        g_top[...] = jnp.zeros_like(g_top)

    @pl.when(me == size - 1)
    def _():
        c_bot[...] = jnp.zeros_like(c_bot)
        g_bot[...] = jnp.zeros_like(g_bot)

    mine = (base + me) // units
    take = remote(place(1), place(1), 0, 1, me)
    pl.when(mine != me)(take.wait_recv)
    for ok, peer, k in ((has_up, me - 1, 2), (has_down, me + 1, 0)):
        copy = remote(place(1), place(k), len(sends), k, peer)
        sends.append((ok, copy))
        pl.when(ok)(copy.start)
    for k in (0, 2):
        remote(place(k), place(k), 0, k, me).wait_recv()
    pl.when(has_up)(remote(c_top, c_top, 0, 4, me).wait_recv)
    pl.when(has_up)(remote(g_top, g_top, 0, 6, me).wait_recv)
    pl.when(has_down)(remote(c_bot, c_bot, 0, 3, me).wait_recv)
    pl.when(has_down)(remote(g_bot, g_bot, 0, 5, me).wait_recv)
    for ok, copy in sends:
        pl.when(ok)(copy.wait_send)


def gather(size, context, cot_context, left, width):
    rows, cols, channels = context.shape
    shapes = [(2, cols, channels)] * 2 + [(1, cols, channels)] * 2 + [(6, width, channels)]
    return pl.pallas_call(
        functools.partial(gather_kernel, size, left, width),
        out_shape=[jax.ShapeDtypeStruct(shape, BF) for shape in shapes],
        in_specs=[pl.BlockSpec(memory_space=pl.ANY)] * 2,
        out_specs=[pl.BlockSpec(memory_space=pltpu.VMEM)] * 5,
        scratch_shapes=[
            pltpu.SemaphoreType.DMA((rows // 2 + 8,)),
            pltpu.SemaphoreType.DMA((7,)),
            pltpu.SemaphoreType.DMA,
        ],
        compiler_params=pltpu.CompilerParams(
            collective_id=0, has_side_effects=True, vmem_limit_bytes=VMEM_LIMIT
        ),
    )(context, cot_context)


def fine_kernel(
    size, lead, crop_ctx, conv_w, bias, proj, blend, blend_t, hr, cot,
    joined, wgrad, parts, crop, upper, acc,
):
    step = pl.program_id(0)
    me = lax.axis_index("rows")
    channels = hr.shape[2]
    cols = hr.shape[1]
    narrow, wide = blend.shape[1], crop_ctx.shape[1]
    chunk = 256

    @pl.when(step == 0)
    def _():
        shifted = []
        for b in range(3):
            total = None
            for a in range(3):
                rows = crop_ctx[pl.ds(a, 4)].reshape(4 * wide, channels)
                term = dot(rows, conv_w[a, b])
                total = term if total is None else total + term
            shifted.append(total.reshape(4, wide, channels))
        for row in range(4):
            pre = bias[...] + sum(
                shifted[b][row, lead + b - 1 : lead + b - 1 + narrow] for b in range(3)
            )
            value = crop_ctx[row + 1, lead : lead + narrow].astype(F32) + pre * sigmoid(pre)
            crop[row] = value.astype(BF)

        @pl.when(me == 0)
        def _():
            crop[0] = crop[1]

        @pl.when(me == size - 1)
        def _():
            crop[3] = crop[2]

        for row in range(4):
            coarse = dot(crop[row], proj[pl.ds(channels, channels)]).astype(BF)
            upper[row] = dot(blend[...], coarse)
        acc[...] = jnp.zeros_like(acc)
        wgrad[...] = jnp.zeros_like(wgrad)

    low = (step + 1) // 2
    start = jnp.where(step % 2 == 0, 9, 1)
    weights = [(2 * k + start).astype(F32) * (1.0 / 16.0) for k in range(4)]

    def body(c, carry):
        at = pl.ds(pl.multiple_of(c * chunk, chunk), chunk)
        lo, hi = upper[low, at], upper[low + 1, at]
        x = hr[:, at].reshape(4 * chunk, channels)
        base = dot(x, proj[pl.ds(0, channels)])
        grads = []
        first = second = None
        for k in range(4):
            v = base[k * chunk : (k + 1) * chunk] + (lo + weights[k] * (hi - lo))
            s = sigmoid(v)
            j = v * s
            joined[k, at] = j.astype(BF)
            g = (cot[k, at].astype(F32) * (s + j * (1.0 - s))).astype(BF)
            grads.append(g)
            g = g.astype(F32)
            part = weights[k] * g
            second = part if second is None else second + part
            rest = g - part
            first = rest if first is None else first + rest
        acc[low, at] += first
        acc[low + 1, at] += second
        wgrad[pl.ds(0, channels)] += t_dot(x, jnp.concatenate(grads, axis=0))
        return carry

    lax.fori_loop(0, cols // chunk, body, 0)

    @pl.when(step == pl.num_programs(0) - 1)
    def _():
        back = [dot(blend_t[...], acc[row].astype(BF)) for row in range(4)]
        top = jnp.where(me == 0, 1.0, 0.0)
        bottom = jnp.where(me == size - 1, 1.0, 0.0)
        back[1] = back[1] + top * back[0]
        back[2] = back[2] + bottom * back[3]
        back = [back[0] * (1.0 - top), back[1], back[2], back[3] * (1.0 - bottom)]
        bottom_w = proj[pl.ds(channels, channels)]
        total = None
        for row in range(4):
            low_back = back[row].astype(BF)
            parts[row] = dot_t(low_back, bottom_w)
            term = t_dot(crop[row], low_back)
            total = term if total is None else total + term
        wgrad[pl.ds(channels, channels)] = total


def fine(size, lead, crop_ctx, conv_weight, conv_bias, proj_weight, hr, cot):
    fine_rows, cols, channels = hr.shape
    narrow = cols // 8
    index = 2 * np.arange(cols) - 7
    lower = index // 16
    frac = ((index - 16 * lower) / 16.0)[:, None]
    column = np.arange(narrow)[None, :]
    left = np.clip(lower, 0, narrow - 1)[:, None]
    right = np.clip(lower + 1, 0, narrow - 1)[:, None]
    blend = (1.0 - frac) * (column == left) + frac * (column == right)
    blend, blend_t = jnp.asarray(blend, BF), jnp.asarray(blend.T, BF)
    whole = lambda shape: pl.BlockSpec(shape, lambda s: (0,) * len(shape))
    tile = pl.BlockSpec((4, cols, channels), lambda s: (s, 0, 0))
    return pl.pallas_call(
        functools.partial(fine_kernel, size, lead),
        grid=(fine_rows // 4,),
        out_shape=[
            jax.ShapeDtypeStruct(hr.shape, BF),
            jax.ShapeDtypeStruct((2 * channels, channels), F32),
            jax.ShapeDtypeStruct((4, narrow, channels), F32),
        ],
        in_specs=[
            whole(crop_ctx.shape),
            whole(conv_weight.shape),
            whole((1, channels)),
            whole(proj_weight.shape),
            whole((cols, narrow)),
            whole((narrow, cols)),
            tile,
            tile,
        ],
        out_specs=[tile, whole((2 * channels, channels)), whole((4, narrow, channels))],
        scratch_shapes=[
            pltpu.VMEM((4, narrow, channels), BF),
            pltpu.VMEM((4, cols, channels), F32),
            pltpu.VMEM((4, cols, channels), F32),
        ],
        compiler_params=pltpu.CompilerParams(vmem_limit_bytes=VMEM_LIMIT),
    )(crop_ctx, conv_weight, conv_bias.reshape(1, -1), proj_weight, blend, blend_t, hr, cot)


def scatter_kernel(
    size, units, parts, ctx, c_top, c_bot, conv_w, bias, out, slope, ext, up, down, got_up, got_down, mine, send, recv, edge,
):
    group, me = enter(size)
    base = 3 * size // 2

    def remote(src, dst, s, r, peer):
        return pltpu.make_async_remote_copy(
            src_ref=src,
            dst_ref=dst,
            send_sem=s,
            recv_sem=r,
            device_id=(group, peer),
            device_id_type=MESH,
        )

    has_up, has_down = me > 0, me < size - 1
    up[...] = parts[0].astype(BF)
    down[...] = parts[3].astype(BF)
    to_up = remote(up, got_down, send.at[0], edge.at[0], me - 1)
    to_down = remote(down, got_up, send.at[1], edge.at[1], me + 1)
    pl.when(has_up)(to_up.start)
    pl.when(has_down)(to_down.start)

    @pl.when(me == 0)
    def _():
        got_up[...] = jnp.zeros_like(got_up)

    @pl.when(me == size - 1)
    def _():
        got_down[...] = jnp.zeros_like(got_down)

    rows, cols, channels = ctx.shape
    ext[pl.ds(0, 2)] = c_top[...]
    ext[pl.ds(2, rows)] = ctx[...]
    ext[pl.ds(rows + 2, 2)] = c_bot[...]
    column = lax.broadcasted_iota(jnp.int32, (cols, channels), 0)

    def forward(p, carry):
        sums = []
        for b in range(3):
            total = None
            for a in range(3):
                term = dot(ext[pl.ds(2 * p + a, 2)].reshape(2 * cols, channels), conv_w[a, b])
                total = term if total is None else total + term
            sums.append(total)
        for k in range(2):
            cut = slice(k * cols, (k + 1) * cols)
            v = bias[...] + jnp.where(column == 0, 0.0, pltpu.roll(sums[0][cut], 1, 0))
            v = v + sums[1][cut]
            v = v + jnp.where(column == cols - 1, 0.0, pltpu.roll(sums[2][cut], cols - 1, 0))
            s = sigmoid(v)
            slope[2 * p + k] = s * (1.0 + v * (1.0 - s))
        return carry

    pairs = (rows + 2) // 2
    lax.fori_loop(0, pairs - 2, forward, 0)

    for s in range(units + 2):
        index = units * me + s - 1 - base

        @pl.when((index < 0) | (index >= size))
        def _():
            out[s] = jnp.zeros_like(out[s])

    pl.when(has_up)(remote(got_up, got_up, send.at[0], edge.at[1], me).wait_recv)
    pl.when(has_down)(remote(got_down, got_down, send.at[0], edge.at[0], me).wait_recv)
    mine[0] = (parts[1] + got_up[...].astype(F32)).astype(BF)
    mine[1] = (parts[2] + got_down[...].astype(F32)).astype(BF)
    number = base + me
    waits = []
    for s in range(units + 2):
        offset = number + 1 - s
        owner = offset // units
        ok = lax.rem(offset, units) == 0
        copy = remote(mine, out.at[s], send.at[2 + s], recv.at[s], owner)
        far = ok & (owner != me) & (owner >= 0) & (owner < size)
        waits.append((far, copy))
        pl.when(far)(copy.start)

        @pl.when(ok & (owner == me))
        def _():
            out[s] = mine[...]

    lax.fori_loop(pairs - 2, pairs, forward, 0)
    for s in range(units + 2):
        index = units * me + s - 1 - base
        here = (index >= 0) & (index < size) & (index != me)
        pl.when(here)(remote(mine, out.at[s], send.at[0], recv.at[s], me).wait_recv)
    for far, copy in waits:
        pl.when(far)(copy.wait_send)
    pl.when(has_up)(to_up.wait_send)
    pl.when(has_down)(to_down.wait_send)


def scatter(size, units, parts, context, c_top, c_bot, conv_weight, conv_bias):
    rows, cols, _ = context.shape
    _, narrow, channels = parts.shape
    row = (narrow, channels)
    return pl.pallas_call(
        functools.partial(scatter_kernel, size, units),
        out_shape=[
            jax.ShapeDtypeStruct((units + 2, 2) + row, BF),
            jax.ShapeDtypeStruct((rows + 2, cols, channels), F32),
        ],
        in_specs=[pl.BlockSpec(memory_space=pltpu.VMEM)] * 6,
        out_specs=[pl.BlockSpec(memory_space=pltpu.VMEM)] * 2,
        scratch_shapes=[pltpu.VMEM((rows + 4, cols, channels), BF)]
        + [pltpu.VMEM(row, BF)] * 4
        + [
            pltpu.VMEM((2,) + row, BF),
            pltpu.SemaphoreType.DMA((units + 4,)),
            pltpu.SemaphoreType.DMA((units + 2,)),
            pltpu.SemaphoreType.DMA((2,)),
        ],
        compiler_params=pltpu.CompilerParams(
            collective_id=1, has_side_effects=True, vmem_limit_bytes=VMEM_LIMIT
        ),
    )(parts, context, c_top, c_bot, conv_weight, conv_bias.reshape(1, -1))


def coarse_kernel(
    left, ctx, c_top, c_bot, cot, g_top, g_bot, crop_grad, conv_w, slope,
    grad, wgrad, bgrad, ext, ext_t, outg, pre_g,
):
    rows, cols, channels = ctx.shape
    narrow = crop_grad.shape[1]
    ext[pl.ds(0, 2)] = c_top[...]
    ext[pl.ds(2, rows)] = ctx[...]
    ext[pl.ds(rows + 2, 2)] = c_bot[...]
    outg[pl.ds(0, 1)] = g_top[...].astype(F32)
    outg[pl.ds(1, rows)] = cot[...].astype(F32)
    outg[pl.ds(rows + 1, 1)] = g_bot[...].astype(F32)
    for r in range(rows + 2):
        outg[r, pl.ds(left, narrow)] += crop_grad[r + 1].astype(F32)
    column = lax.broadcasted_iota(jnp.int32, (cols, channels), 0)

    def later(v):
        return jnp.where(column == 0, 0.0, pltpu.roll(v, 1, 0))

    def sooner(v):
        return jnp.where(column == cols - 1, 0.0, pltpu.roll(v, cols - 1, 0))

    def turn(r, carry):
        ext_t[r] = jnp.transpose(ext[r + 1])
        return carry

    lax.fori_loop(0, rows + 2, turn, 0)
    bgrad[...] = jnp.zeros_like(bgrad)

    def forward(r, carry):
        g = (outg[r] * slope[r]).astype(BF)
        pre_g[1, r] = g
        g = g.astype(F32)
        pre_g[0, r] = sooner(g).astype(BF)
        pre_g[2, r] = later(g).astype(BF)
        own = ((r >= 1) & (r <= rows)).astype(F32)
        bgrad[pl.ds(0, 1)] += own * jnp.sum(g, axis=0, keepdims=True)
        return carry

    lax.fori_loop(0, rows + 2, forward, 0)

    def backward(p, carry):
        sums = []
        for b in range(3):
            total = None
            for a in range(3):
                term = dot_t(
                    pre_g[1, pl.ds(2 * p + 2 - a, 2)].reshape(2 * cols, channels), conv_w[a, b]
                )
                total = term if total is None else total + term
            sums.append(total)
        for k in range(2):
            cut = slice(k * cols, (k + 1) * cols)
            r = 2 * p + k
            grad[r] = outg[r + 1] + (sooner(sums[0][cut]) + sums[1][cut] + later(sums[2][cut]))
        return carry

    lax.fori_loop(0, rows // 2, backward, 0)

    def weights(n, carry):
        a, b = n // 3, n % 3
        total = None
        for i in range(rows):
            term = dot(ext_t[i + a], pre_g[b, i + 1])
            total = term if total is None else total + term
        wgrad[n] = total
        return carry

    lax.fori_loop(0, 9, weights, 0)


def coarse(left, context, halos, cot_context, crop_grad, conv_weight, slope):
    rows, cols, channels = context.shape
    c_top, c_bot, g_top, g_bot = halos
    return pl.pallas_call(
        functools.partial(coarse_kernel, left),
        out_shape=[
            jax.ShapeDtypeStruct((rows, cols, channels), F32),
            jax.ShapeDtypeStruct((9, channels, channels), F32),
            jax.ShapeDtypeStruct((8, channels), F32),
        ],
        in_specs=[pl.BlockSpec(memory_space=pltpu.VMEM)] * 9,
        out_specs=[pl.BlockSpec(memory_space=pltpu.VMEM)] * 3,
        scratch_shapes=[
            pltpu.VMEM((rows + 4, cols, channels), BF),
            pltpu.VMEM((rows + 2, channels, cols), BF),
            pltpu.VMEM((rows + 2, cols, channels), F32),
            pltpu.VMEM((3, rows + 2, cols, channels), BF),
        ],
        compiler_params=pltpu.CompilerParams(vmem_limit_bytes=VMEM_LIMIT),
    )(context, c_top, c_bot, cot_context, g_top, g_bot, crop_grad, conv_weight, slope)


def reduce_kernel(size, conv, proj, bias, out, acc, outgoing, incoming, send, recv, back, load):
    group, me = lax.axis_index("groups"), lax.axis_index("rows")
    total_rows, channels = acc.shape
    half = channels // 2
    bits = [2**k for k in range(size.bit_length() - 1)]
    orders = (bits, bits[:1] + bits[2:] + bits[1:2])
    steps = len(bits)
    n_conv, n_proj, n_bias = conv.shape[0], proj.shape[0], bias.shape[0]
    loads = [
        pltpu.make_async_copy(conv, acc.at[pl.ds(0, n_conv)], load.at[0]),
        pltpu.make_async_copy(proj, acc.at[pl.ds(n_conv, n_proj)], load.at[1]),
        pltpu.make_async_copy(bias, acc.at[pl.ds(n_conv + n_proj, n_bias)], load.at[2]),
    ]
    for copy in loads:
        copy.start()
    used = n_conv + n_proj + n_bias
    acc[pl.ds(used, total_rows - used)] = jnp.zeros((total_rows - used, channels), F32)

    def side(bit):
        return lax.rem(me // bit, 2)

    def partner(bit):
        return me + bit * (1 - 2 * side(bit))

    barrier = pltpu.get_barrier_semaphore()
    for bit in bits:
        pl.semaphore_signal(barrier, inc=1, device_id=(group, partner(bit)), device_id_type=MESH)
    pl.semaphore_wait(barrier, steps)
    for copy in loads:
        copy.wait()

    def remote(src, dst, s, r, bit):
        return pltpu.make_async_remote_copy(
            src_ref=src,
            dst_ref=dst,
            send_sem=s,
            recv_sem=r,
            device_id=(group, partner(bit)),
            device_id_type=MESH,
        )

    def rows_at(start, count):
        return pl.ds(pl.multiple_of(start, 16), count)

    low = [0, 0]
    kept = [[], []]
    copies = []
    pending = [None, None]
    for step in range(steps + 1):
        for h in range(2):
            lanes = pl.ds(h * half, half)
            if step > 0:
                count = total_rows >> step
                pending[h].wait_recv()
                got = incoming[pl.ds(total_rows - 2 * count, count), lanes]
                acc[rows_at(low[h], count), lanes] += got.astype(F32)
            if step < steps:
                bit = orders[h][step]
                count = total_rows >> (step + 1)
                mine = low[h] + side(bit) * count
                other = low[h] + (1 - side(bit)) * count
                there = rows_at(other, count)
                outgoing[there, lanes] = acc[there, lanes].astype(BF)
                copy = remote(
                    outgoing.at[there, lanes],
                    incoming.at[pl.ds(total_rows - 2 * count, count), lanes],
                    send.at[h, step],
                    recv.at[h, step],
                    bit,
                )
                copy.start()
                copies.append(copy)
                pending[h] = copy
                low[h] = mine
                kept[h].append(mine)
            else:
                here = rows_at(low[h], total_rows >> steps)
                out[here, lanes] = acc[here, lanes].astype(BF)
                bit = orders[h][steps - 1]
                copy = remote(
                    out.at[here, lanes],
                    out.at[here, lanes],
                    send.at[h, steps],
                    back.at[h, steps - 1],
                    bit,
                )
                copy.start()
                copies.append(copy)
                pending[h] = copy
    for step in reversed(range(steps)):
        for h in range(2):
            lanes = pl.ds(h * half, half)
            pending[h].wait_recv()
            if step > 0:
                here = rows_at(kept[h][step - 1], total_rows >> step)
                copy = remote(
                    out.at[here, lanes],
                    out.at[here, lanes],
                    send.at[h, 2 * steps - step],
                    back.at[h, step - 1],
                    orders[h][step - 1],
                )
                copy.start()
                copies.append(copy)
                pending[h] = copy
    for copy in copies:
        copy.wait_send()


def reduce_sums(size, conv, proj, bias):
    channels = conv.shape[1]
    rows = conv.shape[0] + proj.shape[0] + bias.shape[0]
    rows = -(-rows // (16 * size)) * 16 * size
    steps = size.bit_length() - 1
    return pl.pallas_call(
        functools.partial(reduce_kernel, size),
        out_shape=jax.ShapeDtypeStruct((rows, channels), BF),
        in_specs=[pl.BlockSpec(memory_space=pl.ANY)] * 3,
        out_specs=pl.BlockSpec(memory_space=pltpu.VMEM),
        scratch_shapes=[
            pltpu.VMEM((rows, channels), F32),
            pltpu.VMEM((rows, channels), BF),
            pltpu.VMEM((rows, channels), BF),
            pltpu.SemaphoreType.DMA((2, 2 * steps)),
            pltpu.SemaphoreType.DMA((2, steps)),
            pltpu.SemaphoreType.DMA((2, steps)),
            pltpu.SemaphoreType.DMA((3,)),
        ],
        compiler_params=pltpu.CompilerParams(
            collective_id=2, has_side_effects=True, vmem_limit_bytes=VMEM_LIMIT
        ),
    )(conv, proj, bias)


def widen_kernel(sums, conv, proj, bias):
    n_conv, n_proj = conv.shape[0], proj.shape[0]
    step = 256

    def body(n, carry):
        at = pl.ds(pl.multiple_of(n * step, step), step)
        conv[at] = sums[at].astype(F32)
        return carry

    lax.fori_loop(0, n_conv // step, body, 0)
    proj[...] = sums[pl.ds(n_conv, n_proj)].astype(F32)
    bias[...] = sums[pl.ds(n_conv + n_proj, 16)].astype(F32)[:1]


def widen(sums):
    channels = sums.shape[1]
    return pl.pallas_call(
        widen_kernel,
        out_shape=[jax.ShapeDtypeStruct((n, channels), F32) for n in (9 * channels, 2 * channels, 1)],
        in_specs=[pl.BlockSpec(memory_space=pltpu.VMEM)],
        out_specs=[pl.BlockSpec(memory_space=pltpu.VMEM)] * 3,
        compiler_params=pltpu.CompilerParams(vmem_limit_bytes=VMEM_LIMIT),
    )(sums)


def per_device(size, context, conv_weight, conv_bias, hr_features, proj_weight, cot_joined,
               cot_context):
    rows, cols, channels = context.shape
    narrow = hr_features.shape[1] // 8
    left = (cols - narrow) // 2
    lead = 16
    *halos, crop_ctx = gather(size, context, cot_context, left - lead, narrow + 2 * lead)
    joined, proj_grad, parts = fine(
        size, lead, crop_ctx, conv_weight, conv_bias, proj_weight, hr_features, cot_joined
    )
    crop_grad, slope = scatter(
        size, rows // 2, parts, context, *halos[:2], conv_weight, conv_bias
    )
    crop_grad = crop_grad.reshape(-1, narrow, channels)
    grad, conv_grad, bias_grad = coarse(
        left, context, halos, cot_context, crop_grad, conv_weight, slope
    )
    conv_sum, proj_sum, bias_sum = widen(
        reduce_sums(size, conv_grad.reshape(-1, channels), proj_grad, bias_grad)
    )
    return (
        joined,
        grad,
        conv_sum.reshape(3, 3, channels, channels),
        bias_sum.reshape(-1),
        proj_sum,
    )


def solution(mesh):
    tile = P(("groups", "rows"), None, None)
    return jax.shard_map(
        functools.partial(per_device, mesh.shape["rows"]),
        mesh=mesh,
        in_specs=(tile, P(), P(), tile, P(), tile, tile),
        out_specs=(tile, tile, P("groups", None, None, None), P("groups"), P("groups", None)),
        check_vma=False,
    )
```
